256 devices in a mesh: gx: 32 (over z_hi, x, core), gz: 8 (over y, z_lo).
Axes of the slice: x: 4, y: 4, z: 8 (z_hi: 4, z_lo: 2; z = z_hi * 2 + z_lo), core: 2. Of those that a mesh axis runs over, the one named last changes fastest.
Arguments:
- velocity: float32 [2048, 16, 1024], P('gx', None, 'gz'), may hold values from -6 to 6
- stress_xz: float32 [2, 2048, 16, 1024], P(None, 'gx', None, 'gz'), may hold values from -6 to 6
- stress_y: float32 [2048, 15, 1024], P('gx', None, 'gz'), may hold values from -6 to 6
- rigidity: float32 [2048, 16, 1024], P('gx', None, 'gz'), may hold values from 0.5 to 2
- buoyancy: float32 [2048, 16, 1024], P('gx', None, 'gz'), may hold values from 0.5 to 2
- sigma_star: float32 [2048, 1024], P('gx', 'gz'), may hold values from 1 to 3
- sigma_zero: float32 [2048, 1024], P('gx', 'gz'), may hold values from 1 to 3
- friction: float32 [2048, 1024], P('gx', 'gz'), may hold values from 0.3 to 0.8
- history: bfloat16 [2, 64, 2048, 1024], P(None, None, 'gx', 'gz'), may hold values from -6 to 6
- kernel: bfloat16 [2, 5, 64, 4096], replicated, may hold values from -0.09375 to 0.09375
- cone: int32 [2, 32, 5, 2], replicated, may hold values from 0 to 64, as said below
Outputs:
- new_velocity: float32 [2048, 16, 1024], P('gx', None, 'gz')
- new_stress_xz: float32 [2, 2048, 16, 1024], P(None, 'gx', None, 'gz')
- new_stress_y: float32 [2048, 15, 1024], P('gx', None, 'gz')
- new_state: float32 [2048, 1024], P('gx', 'gz')
- boundary_traction: float32 [2, 2048, 1024], P(None, 'gx', 'gz')
The draws below stay inside these ranges and needn't reach their ends.
Inputs may be any that keep to these rules, and one draw needn't show every extreme that they name: cone[s, b, o] holds (first lag, end of lags) for source block b - (o - 2); a pair outside the light cone or whose source lies outside the blocks holds (0, 0); offset 0 always holds (0, 64); offsets -1 and 1 with a source inside the blocks always hold first lag 0; otherwise first lag < end of lags.
All inputs are finite; a program needn't handle non-finite values.
Results may differ from the reference program's by a relative error of at most 0.0022.
Values may be sent and summed in bfloat16 or wider, within the bound.
No kernel may reach another device: no remote copies, remote signals or barrier semaphores. Data moves between devices by JAX's collectives and lax.ppermute only.
A program may use at most 128 MiB of HBM per device.

```python
import math
import jax
import jax.numpy as jnp
from jax import lax

CX = 64
NY = 16
LAGS = 64
REACH = 2
NOFF = 5
BLOCKS = 32
NX = 2048
NZ = 1024
N_GX = 32


def draw_cone(key, part):
    key = jax.random.fold_in(key, 7)
    key_reach, key_first, key_last = jax.random.split(key, 3)
    offset = jnp.arange(NOFF, dtype=jnp.int32) - REACH
    target = jnp.arange(BLOCKS, dtype=jnp.int32)
    source = target[:, None] - offset[None, :]
    inside = (source >= 0) & (source < BLOCKS)
    reach_block = jax.random.randint(key_reach, (2, BLOCKS, 1), 1, REACH + 1)
    distance = jnp.abs(offset)[None, None, :]
    active = inside[None] & (distance <= reach_block)
    first = jnp.maximum(distance - 1, 0) * 12 + jax.random.randint(key_first, (2, BLOCKS, NOFF), 0, 12)
    first = jnp.where(distance <= 1, 0, first)
    last = LAGS - jax.random.randint(key_last, (2, BLOCKS, NOFF), 0, 8)
    last = jnp.where(offset[None, None, :] == 0, LAGS, last)
    first = jnp.where(active, first, 0)
    last = jnp.where(active, last, 0)
    return jnp.stack([first, last], axis=-1).astype(jnp.int32)


def steps_of(stream_key, extent, cuts, least, high):
    factor_of = 1.0
    for position, shards_of in cuts:
        draws = jax.random.uniform(jax.random.fold_in(jax.random.fold_in(stream_key, 6), position), (shards_of,), jnp.float32, least / len(cuts), high / len(cuts))
        factor_of = factor_of * jnp.repeat(jnp.exp(draws), extent[position] // shards_of).reshape((-1,) + (1,) * (len(extent) - 1 - position))
    return factor_of


def noise(own_key, extent, width, limit, cuts=(), held_as=jnp.bfloat16):
    loudness = steps_of(own_key, extent, cuts, -0.22, 0.18) if cuts else 1.0
    entries = jax.random.normal(own_key, extent, jnp.float32) * width * loudness
    return jnp.minimum(jnp.maximum(entries, -limit), limit).astype(held_as)


def setup_inputs(seed: int = 0) -> dict:
    keys = jax.random.split(jax.random.key(seed), 12)
    return {
        "velocity": noise(keys[0], (NX, NY, NZ), 1.0, 6.0, ((0, 32), (2, 8)), jnp.float32),
        "stress_xz": noise(keys[1], (2, NX, NY, NZ), 1.0, 6.0, ((1, 32), (3, 8)), jnp.float32),
        "stress_y": noise(keys[2], (NX, NY - 1, NZ), 1.0, 6.0, ((0, 32), (2, 8)), jnp.float32),
        "rigidity": jnp.clip(jnp.exp(math.log(2.0) - 1.3862944 * jax.random.uniform(keys[3], (NX, NY, NZ), jnp.float32) ** steps_of(keys[3], (NX, NY, NZ), ((0, 32), (2, 8)), -0.2, 0.2)), 0.5, 2.0),
        "buoyancy": jnp.clip(jnp.exp(math.log(2.0) - 1.3862944 * jax.random.uniform(keys[4], (NX, NY, NZ), jnp.float32) ** steps_of(keys[4], (NX, NY, NZ), ((0, 32), (2, 8)), -0.2, 0.2)), 0.5, 2.0),
        "sigma_star": jnp.clip(1.0 + 2.0 * jax.random.uniform(keys[5], (NX, NZ), jnp.float32) ** steps_of(keys[5], (NX, NZ), ((0, 32), (1, 8)), -0.2, 0.2), 1.0, 3.0),
        "sigma_zero": jnp.clip(1.0 + 2.0 * jax.random.uniform(keys[6], (NX, NZ), jnp.float32) ** steps_of(keys[6], (NX, NZ), ((0, 32), (1, 8)), -0.2, 0.2), 1.0, 3.0),
        "friction": jnp.clip(0.3 + 0.5 * jax.random.uniform(keys[7], (NX, NZ), jnp.float32) ** steps_of(keys[7], (NX, NZ), ((0, 32), (1, 8)), -0.2, 0.2), 0.3, 0.8),
        "history": noise(keys[8], (2, LAGS, NX, NZ), 1.0, 6.0, ((2, 32), (3, 8))),
        "kernel": noise(keys[9], (2, NOFF, CX, LAGS * CX), (LAGS * CX) ** -0.5, 0.09375),
        "cone": draw_cone(jax.random.fold_in(keys[11], 71), 0),
    }


courant = 0.25
bimaterial = 0.5
slip_ref = 0.2
decay_rate = 0.5
impedance = 0.5


def shift_blocks(blocked, offset):
    if offset == 0:
        return blocked
    if offset > 0:
        return jnp.concatenate([jnp.zeros_like(blocked[:, :, :offset]), blocked[:, :, :-offset]], axis=2)
    return jnp.concatenate([blocked[:, :, -offset:], jnp.zeros_like(blocked[:, :, :(-offset)])], axis=2)


def cone_term(history, kernel, cone):
    blocked = history.reshape(2, LAGS, N_GX, CX, history.shape[3])
    lag_index = jnp.arange(LAGS, dtype=jnp.int32)
    totals = [jnp.zeros((N_GX, CX, history.shape[3]), jnp.float32) for surface in range(2)]
    for index in range(NOFF):
        source = shift_blocks(blocked, index - REACH)
        first = cone[:, :, index, 0]
        last = cone[:, :, index, 1]
        keep = ((lag_index[None, None, :] >= first[:, :, None]) & (lag_index[None, None, :] < last[:, :, None])).astype(jnp.bfloat16)
        for surface in range(2):
            masked = source[surface] * jnp.transpose(keep[surface])[:, :, None, None]
            matrix = kernel[surface, index].reshape(CX, LAGS, CX).astype(jnp.float32)
            part = jnp.einsum('xky,kbyz->bxz', matrix, masked.astype(jnp.float32), precision=lax.Precision.HIGHEST)
            totals[surface] = totals[surface] + part
    return jnp.stack(totals).reshape(2, N_GX * CX, history.shape[3])


def advance(velocity, stress_xz, stress_y, rigidity, buoyancy, sigma_star, sigma_zero, friction, traction_history):
    padded = jnp.pad(velocity, ((1, 1), (0, 0), (1, 1)))
    along_x = padded[2:, :, 1:-1] - padded[:-2, :, 1:-1]
    along_z = padded[1:-1, :, 2:] - padded[1:-1, :, :-2]
    stress_x = stress_xz[0] + courant * 0.5 * rigidity * along_x
    stress_z = stress_xz[1] + courant * 0.5 * rigidity * along_z
    face_rigidity = 0.5 * (rigidity[:, 1:] + rigidity[:, :-1])
    trial = stress_y + courant * face_rigidity * (velocity[:, 1:] - velocity[:, :-1])
    fault = velocity.shape[1] // 2 - 1
    slip_rate = velocity[:, fault + 1] - velocity[:, fault]
    normal = sigma_zero + bimaterial * jnp.tanh(stress_x[:, fault + 1] - stress_x[:, fault])
    state = normal + (sigma_star - normal) * jnp.exp(-(jnp.abs(slip_rate) + slip_ref) * decay_rate)
    strength = friction * state
    stress_y_new = trial.at[:, fault].set(jnp.clip(trial[:, fault], -strength, strength))
    bottom = traction_history[0] + impedance * velocity[:, 0]
    top = traction_history[1] - impedance * velocity[:, -1]
    stacked = jnp.stack([stress_x, stress_z])
    spread = jnp.pad(stacked, ((0, 0), (1, 1), (0, 0), (1, 1)))
    divergence = 0.5 * (spread[0, 2:, :, 1:-1] - spread[0, :-2, :, 1:-1]) + 0.5 * (spread[1, 1:-1, :, 2:] - spread[1, 1:-1, :, :-2])
    faces = jnp.concatenate([bottom[:, None], stress_y_new, top[:, None]], axis=1)
    velocity_new = velocity + courant * buoyancy * (divergence + faces[:, 1:] - faces[:, :-1])
    return velocity_new, stacked, stress_y_new, state, jnp.stack([bottom, top])


def reference(velocity, stress_xz, stress_y, rigidity, buoyancy, sigma_star, sigma_zero, friction, history, kernel, cone):
    traction_one = cone_term(history, kernel, cone)
    velocity_one, stress_one, face_one, state_one, bounds_one = advance(velocity, stress_xz, stress_y, rigidity, buoyancy, sigma_star, sigma_zero, friction, traction_one)
    newest = jnp.stack([velocity_one[:, 0], velocity_one[:, -1]]).astype(jnp.bfloat16)
    history_next = jnp.concatenate([newest[:, None], history[:, :-1]], axis=1)
    traction_two = cone_term(history_next, kernel, cone)
    return advance(velocity_one, stress_one, face_one, rigidity, buoyancy, state_one, sigma_zero, friction, traction_two)
```

```python
import functools
import jax
import jax.numpy as jnp
from jax import lax
from jax.experimental import pallas as pl
from jax.experimental.pallas import tpu as pltpu
from jax.sharding import PartitionSpec as P

courant = 0.25
bimaterial = 0.5
slip_ref = 0.2
decay_rate = 0.5
impedance = 0.5

GX, GZ = "gx", "gz"
CHUNK = 8
LAG_CHUNK = 16
MIB = 2**20


def swap_pairs(axis, distance, phase):
    size, pairs = lax.axis_size(axis), []
    for i in range(size):
        partner = i + distance if (i - phase) % (2 * distance) < distance else i - distance
        if 0 <= partner < size:
            pairs.append((i, partner))
    return pairs


def parities():
    block = lax.axis_index(GX)
    even = lax.rem(block, 2) == 0
    chip_even = lax.rem(lax.div(block, 2), 2) == 0
    depth_even = lax.rem(lax.axis_index(GZ), 2) == 0
    return even, chip_even, depth_even


def lane_of(shape):
    return lax.broadcasted_iota(jnp.int32, shape, len(shape) - 1)


def turned(value, shift):
    return pltpu.roll(value, shift % value.shape[-1], value.ndim - 1)


def depth_edges(velocity, stress_z, rigidity):
    lane = lane_of(velocity.shape)
    count = velocity.shape[-1]
    after = jnp.where(lane == count - 1, 0.0, turned(velocity, -1))
    before = jnp.where(lane == 0, 0.0, turned(velocity, 1))
    partial = stress_z + courant * 0.5 * rigidity * (after - before)
    packed = jnp.where(
        lane < 2, turned(velocity, 1), jnp.where(lane < 4, turned(rigidity, 3), turned(partial, 5))
    )
    return packed.reshape(-1, count).T[:8]


def first_kernel(
    cone, history, kernel, velocity, stress, rigidity, core, own, later, lead, edges, total, tail
):
    surface, part = pl.program_id(0), pl.program_id(1)
    parts = pl.num_programs(1)
    nodes = own.shape[1] // 3
    offsets = kernel.shape[1] // nodes
    reach = (offsets - 1) // 2
    columns = kernel.shape[2]
    blocks = cone.shape[3]
    block = lax.axis_index(GX)

    lag = lax.div(lane_of((1, columns)), nodes) + part * (columns // nodes)
    masked = []
    for index in range(offsets):
        target = jnp.clip(block + (index - reach), 0, blocks - 1)
        first, last = cone[surface, index, 0, target], cone[surface, index, 1, target]
        keep = jnp.where((lag >= first) & (lag < last), 1.0, 0.0).astype(jnp.bfloat16)
        masked.append(kernel[0, index * nodes : (index + 1) * nodes, :] * keep)
    matrix = jnp.concatenate(masked, axis=0)

    @pl.when(part == 0)
    def _():
        tail[...] = jnp.zeros_like(tail)
        total[...] = jnp.zeros_like(total)
        lead[0] = matrix[:, :nodes]

    now = history[0]
    shifted = jnp.concatenate([tail[...], now[: columns - nodes]], axis=0)
    both = jnp.concatenate([now, shifted], axis=1)
    total[...] += jnp.dot(matrix, both, preferred_element_type=jnp.float32)
    tail[...] = now[columns - nodes :]

    @pl.when(part == parts - 1)
    def _():
        width = now.shape[1]
        for place, index in enumerate((0, 2, 4)):
            own[0, place * nodes : (place + 1) * nodes] = total[
                index * nodes : (index + 1) * nodes, :width
            ]
        base = pl.multiple_of(surface * (2 * nodes), 2 * nodes)
        core[pl.ds(base, nodes), :] = total[nodes : 2 * nodes, :width]
        core[pl.ds(base + nodes, nodes), :] = total[3 * nodes : 4 * nodes, :width]
        later[0] = total[:, width:]

    step = surface * parts + part
    width = velocity.shape[0] * velocity.shape[1]
    edges[:, pl.ds(pl.multiple_of(step * width, width), width)] = depth_edges(
        velocity[...], stress[1], rigidity[...]
    )

    @pl.when(step == 0)
    def _():
        strike_edge(core, 4 * nodes, velocity[0], rigidity[0], stress[0, 0], velocity[1], 1.0)

    @pl.when(step == pl.num_programs(0) * parts - 1)
    def _():
        n = velocity.shape[0]
        strike_edge(
            core,
            4 * nodes + 48,
            velocity[n - 1],
            rigidity[n - 1],
            stress[0, n - 1],
            velocity[n - 2],
            -1.0,
        )


def strike_edge(core, base, velocity, rigidity, stress_x, inner, sign):
    core[base : base + 16] = velocity
    core[base + 16 : base + 32] = rigidity
    core[base + 32 : base + 48] = stress_x + (sign * courant * 0.5) * rigidity * inner


def first_call(cone, history, kernel, velocity, stress, rigidity):
    surfaces, rows, columns = kernel.shape
    nodes = velocity.shape[0]
    width = history.shape[2]
    chunk = LAG_CHUNK * nodes
    parts = columns // chunk
    slab = nodes // (surfaces * parts)
    ny = velocity.shape[1]
    f32 = jnp.float32
    return pl.pallas_call(
        first_kernel,
        grid=(surfaces, parts),
        in_specs=[
            pl.BlockSpec(memory_space=pltpu.SMEM),
            pl.BlockSpec((1, chunk, width), lambda s, k: (s, k, 0)),
            pl.BlockSpec((1, rows, chunk), lambda s, k: (s, 0, k)),
            pl.BlockSpec((slab, ny, width), lambda s, k: (s * parts + k, 0, 0)),
            pl.BlockSpec((2, slab, ny, width), lambda s, k: (0, s * parts + k, 0, 0)),
            pl.BlockSpec((slab, ny, width), lambda s, k: (s * parts + k, 0, 0)),
        ],
        out_specs=[
            pl.BlockSpec((4 * nodes + 96, width), lambda s, k: (0, 0)),
            pl.BlockSpec((1, 3 * nodes, width), lambda s, k: (s, 0, 0)),
            pl.BlockSpec((1, rows, width), lambda s, k: (s, 0, 0)),
            pl.BlockSpec((1, rows, nodes), lambda s, k: (s, 0, 0)),
            pl.BlockSpec((8, nodes * ny), lambda s, k: (0, 0)),
        ],
        out_shape=[
            jax.ShapeDtypeStruct((4 * nodes + 96, width), f32),
            jax.ShapeDtypeStruct((surfaces, 3 * nodes, width), f32),
            jax.ShapeDtypeStruct((surfaces, rows, width), f32),
            jax.ShapeDtypeStruct((surfaces, rows, nodes), jnp.bfloat16),
            jax.ShapeDtypeStruct((8, nodes * ny), f32),
        ],
        scratch_shapes=[
            pltpu.VMEM((rows, 2 * width), f32),
            pltpu.VMEM((nodes, width), jnp.bfloat16),
        ],
        compiler_params=pltpu.CompilerParams(vmem_limit_bytes=16 * MIB),
    )(cone, history, kernel, velocity, stress, rigidity)


def relay_kernel(received, own, near, far):
    even, chip_even, _ = parities()
    nodes = own.shape[1] // 3
    right, left = [], []
    for surface in range(2):
        base = surface * 2 * nodes
        from_left = received[base : base + nodes]
        from_right = received[base + nodes : base + 2 * nodes]
        nothing = jnp.zeros_like(from_left)
        left.append(own[surface, :nodes] + lax.select(even, nothing, from_left))
        right.append(own[surface, 2 * nodes :] + lax.select(even, from_right, nothing))
    left.append(received[4 * nodes : 4 * nodes + 48])
    right.append(received[4 * nodes + 48 :])
    base = 0
    for to_left, to_right in zip(left, right):
        size = to_left.shape[0]
        near[base : base + size] = lax.select(chip_even, to_right, to_left)
        far[base : base + size] = lax.select(chip_even, to_left, to_right)
        base += size


def relay_call(received, own):
    nodes, width = own.shape[1] // 3, own.shape[2]
    shape = jax.ShapeDtypeStruct((2 * nodes + 48, width), jnp.float32)
    return pl.pallas_call(
        relay_kernel,
        out_shape=[shape, shape],
        compiler_params=pltpu.CompilerParams(vmem_limit_bytes=4 * MIB),
    )(received, own)


def step_kernel(last, *refs):
    (velocity, stress, stress_y, rigidity, buoyancy, sigma_star, sigma_zero, friction) = refs[:8]
    (received, near, far, depth_near, depth_far, own) = refs[8:14]
    refs = refs[14:]
    if last:
        velocity_new, stress_new, stress_y_new, state_new, bounds = refs[:5]
        refs = refs[5:]
    else:
        later, lead = refs[:2]
        velocity_new, stress_new, stress_y_new, state_new, core, own_new, edges = refs[2:9]
        refs = refs[9:]
    padded, spread, depth, partial, traction = refs[:5]
    even, chip_even, depth_even = parities()
    nodes, ny, width = velocity.shape
    fault = ny // 2 - 1
    scale = courant * 0.5

    for surface in range(2):
        base = surface * 2 * nodes
        mate = lax.select(
            even, received[base : base + nodes], received[base + nodes : base + 2 * nodes]
        )
        rows = slice(surface * nodes, (surface + 1) * nodes)
        traction[surface] = own[surface, nodes : 2 * nodes] + mate + near[rows] + far[rows]

    near_halo, far_halo = near[2 * nodes :], far[2 * nodes :]
    left = lax.select(
        even, lax.select(chip_even, far_halo, near_halo), received[4 * nodes + 48 :]
    )
    right = lax.select(
        even, received[4 * nodes : 4 * nodes + 48], lax.select(chip_even, near_halo, far_halo)
    )
    padded[0], padded[nodes + 1] = left[:16], right[:16]
    spread[0] = left[32:] + scale * left[16:32] * velocity[0]
    spread[nodes + 1] = right[32:] - scale * right[16:32] * velocity[nodes - 1]

    from_left = lax.select(depth_even, depth_far[...], depth_near[...])
    from_right = lax.select(depth_even, depth_near[...], depth_far[...])
    row = lax.broadcasted_iota(jnp.int32, from_left.shape, 0)
    depth[...] = jnp.where(
        lax.rem(row, 2) == 0, pltpu.roll(from_right, 7, 0), pltpu.roll(from_left, 1, 0)
    )

    def fill(i, carry):
        at = i * CHUNK
        padded[pl.ds(at + 1, CHUNK)] = velocity[pl.ds(at, CHUNK)]
        return carry

    lax.fori_loop(0, nodes // CHUNK, fill, 0)

    shape = (CHUNK, ny, width)
    lane = lane_of(shape)
    level = lax.broadcasted_iota(jnp.int32, shape, 1)

    def stresses(i, carry):
        at = pl.multiple_of(i * CHUNK, CHUNK)
        cells = pl.ds(at, CHUNK)
        here, rigid = velocity[cells], rigidity[cells]
        stress_x = stress[0, cells] + scale * rigid * (
            padded[pl.ds(at + 2, CHUNK)] - padded[cells]
        )
        spread[pl.ds(at + 1, CHUNK)] = stress_x
        stress_new[0, cells] = stress_x

        halo = depth[:, pl.ds(pl.multiple_of(i * CHUNK * ny, CHUNK * ny), CHUNK * ny)]
        halo = jnp.concatenate([halo, jnp.zeros((width - 8, CHUNK * ny), jnp.float32)], axis=0)
        halo = halo.T.reshape(shape)
        sides = turned(halo, -1)
        after = jnp.where(lane == width - 1, sides, turned(here, -1))
        before = jnp.where(lane == 0, sides, turned(here, 1))
        stress_z = stress[1, cells] + scale * rigid * (after - before)
        stress_new[1, cells] = stress_z
        change = scale * turned(halo, -3) * here
        sides = turned(halo, -5) + jnp.where(lane == 0, change, -change)
        after = jnp.where(lane == width - 1, sides, turned(stress_z, -1))
        before = jnp.where(lane == 0, sides, turned(stress_z, 1))
        spreading = 0.5 * (after - before)

        faces = stress_y[cells]
        faces = faces[:, : ny - 1]
        trial = faces + courant * (0.5 * (rigid[:, 1:] + rigid[:, :-1])) * (
            here[:, 1:] - here[:, :-1]
        )
        slip_rate = here[:, fault + 1] - here[:, fault]
        zero = sigma_zero[cells]
        normal = zero + bimaterial * jnp.tanh(stress_x[:, fault + 1] - stress_x[:, fault])
        state = normal + (sigma_star[cells] - normal) * jnp.exp(
            -(jnp.abs(slip_rate) + slip_ref) * decay_rate
        )
        state_new[cells] = state
        strength = friction[cells] * state
        clipped = jnp.clip(trial[:, fault], -strength, strength)
        bottom = traction[0, cells] + impedance * here[:, 0]
        top = traction[1, cells] - impedance * here[:, ny - 1]
        if last:
            bounds[0, cells] = bottom
            bounds[1, cells] = top
        above = jnp.concatenate([trial, top[:, None]], axis=1)
        above = jnp.where(level == fault, clipped[:, None], above)
        stress_y_new[cells] = above[:, : stress_y_new.shape[1]]
        below = jnp.where(level == 0, bottom[:, None], pltpu.roll(above, 1, 1))
        partial[cells] = spreading + above - below
        return carry

    lax.fori_loop(0, nodes // CHUNK, stresses, 0)

    def velocities(i, carry):
        at = pl.multiple_of(i * CHUNK, CHUNK)
        cells = pl.ds(at, CHUNK)
        along = 0.5 * (spread[pl.ds(at + 2, CHUNK)] - spread[cells])
        moved = velocity[cells] + courant * buoyancy[cells] * (along + partial[cells])
        velocity_new[cells] = moved
        if not last:
            newest = refs[5]
            newest[0, cells] = moved[:, 0]
            newest[1, cells] = moved[:, ny - 1]
            edges[:, pl.ds(pl.multiple_of(i * CHUNK * ny, CHUNK * ny), CHUNK * ny)] = depth_edges(
                moved, stress_new[1, cells], rigidity[cells]
            )
        return carry

    lax.fori_loop(0, nodes // CHUNK, velocities, 0)

    if not last:
        newest = refs[5]
        for surface in range(2):
            fresh = newest[surface].astype(jnp.bfloat16)
            total = later[surface] + jnp.dot(
                lead[surface], fresh, preferred_element_type=jnp.float32
            )
            for place, index in enumerate((0, 2, 4)):
                own_new[surface, place * nodes : (place + 1) * nodes] = total[
                    index * nodes : (index + 1) * nodes
                ]
            base = surface * 2 * nodes
            core[base : base + nodes] = total[nodes : 2 * nodes]
            core[base + nodes : base + 2 * nodes] = total[3 * nodes : 4 * nodes]
        strike_edge(
            core, 4 * nodes, velocity_new[0], rigidity[0], stress_new[0, 0], velocity_new[1], 1.0
        )
        strike_edge(
            core,
            4 * nodes + 48,
            velocity_new[nodes - 1],
            rigidity[nodes - 1],
            stress_new[0, nodes - 1],
            velocity_new[nodes - 2],
            -1.0,
        )


def step_call(last, *args):
    nodes, ny, width = args[0].shape
    f32 = jnp.float32

    def shaped(*shape):
        return jax.ShapeDtypeStruct(shape, f32)

    outs = [
        shaped(nodes, ny, width),
        shaped(2, nodes, ny, width),
        shaped(nodes, ny - 1 if last else ny, width),
        shaped(nodes, width),
    ]
    if last:
        outs += [shaped(2, nodes, width)]
    else:
        outs += [
            shaped(4 * nodes + 96, width),
            shaped(2, 3 * nodes, width),
            shaped(8, nodes * ny),
        ]
    scratch = [
        pltpu.VMEM((nodes + 2, ny, width), f32),
        pltpu.VMEM((nodes + 2, ny, width), f32),
        pltpu.VMEM((8, nodes * ny), f32),
        pltpu.VMEM((nodes, ny, width), f32),
        pltpu.VMEM((2, nodes, width), f32),
    ]
    if not last:
        scratch += [pltpu.VMEM((2, nodes, width), f32)]
    return pl.pallas_call(
        functools.partial(step_kernel, last),
        out_shape=outs,
        scratch_shapes=scratch,
        compiler_params=pltpu.CompilerParams(vmem_limit_bytes=24 * MIB),
    )(*args)


def exchange(core, own, edges):
    received = lax.ppermute(core, GX, swap_pairs(GX, 1, 0))
    near, far = relay_call(received, own)
    far = lax.ppermute(far, GX, swap_pairs(GX, 2, 2))
    near = lax.ppermute(near, GX, swap_pairs(GX, 2, 0))
    depth_far = lax.ppermute(edges, GZ, swap_pairs(GZ, 1, 1))
    depth_near = lax.ppermute(edges, GZ, swap_pairs(GZ, 1, 0))
    return received, near, far, depth_near, depth_far


def local(
    velocity,
    stress_xz,
    stress_y,
    rigidity,
    buoyancy,
    sigma_star,
    sigma_zero,
    friction,
    history,
    kernel,
    cone,
):
    surfaces, lags, nodes, width = history.shape
    past = history.reshape(surfaces, lags * nodes, width)
    matrix = kernel.reshape(surfaces, -1, kernel.shape[3])
    turned_cone = jnp.transpose(cone, (0, 2, 3, 1))
    core, own, later, lead, edges = first_call(
        turned_cone, past, matrix, velocity, stress_xz, rigidity
    )
    moved = exchange(core, own, edges)
    velocity, stress_xz, stress_y, state, core, own, edges = step_call(
        False,
        velocity,
        stress_xz,
        stress_y,
        rigidity,
        buoyancy,
        sigma_star,
        sigma_zero,
        friction,
        *moved,
        own,
        later,
        lead,
    )
    moved = exchange(core, own, edges)
    return step_call(
        True,
        velocity,
        stress_xz,
        stress_y,
        rigidity,
        buoyancy,
        state,
        sigma_zero,
        friction,
        *moved,
        own,
    )


def solution(mesh):
    in_specs = (
        P("gx", None, "gz"),
        P(None, "gx", None, "gz"),
        P("gx", None, "gz"),
        P("gx", None, "gz"),
        P("gx", None, "gz"),
        P("gx", "gz"),
        P("gx", "gz"),
        P("gx", "gz"),
        P(None, None, "gx", "gz"),
        P(),
        P(),
    )
    out_specs = (
        P("gx", None, "gz"),
        P(None, "gx", None, "gz"),
        P("gx", None, "gz"),
        P("gx", "gz"),
        P(None, "gx", "gz"),
    )
    return jax.shard_map(
        local, mesh=mesh, in_specs=in_specs, out_specs=tuple(out_specs), check_vma=False
    )
```

```python
import functools

import jax
import jax.numpy as jnp
from jax import lax
from jax.experimental import pallas as pl
from jax.experimental.pallas import tpu as pltpu
from jax.sharding import PartitionSpec as P

courant = 0.25
bimaterial = 0.5
slip_ref = 0.2
decay_rate = 0.5
impedance = 0.5

GX, GZ = "gx", "gz"
CHUNK = 8
CHUNK_COLUMNS = 1024
SPARE = 8
MIB = 2**20
FIRST_LIMIT = 12 * MIB


def swap_pairs(axis, distance, phase):
    size, pairs = lax.axis_size(axis), []
    for i in range(size):
        partner = i + distance if (i - phase) % (2 * distance) < distance else i - distance
        if 0 <= partner < size:
            pairs.append((i, partner))
    return pairs


def parities():
    block = lax.axis_index(GX)
    even = lax.rem(block, 2) == 0
    chip_even = lax.rem(lax.div(block, 2), 2) == 0
    depth_even = lax.rem(lax.axis_index(GZ), 2) == 0
    return even, chip_even, depth_even


def lane_of(shape):
    return lax.broadcasted_iota(jnp.int32, shape, len(shape) - 1)


def turned(value, shift):
    return pltpu.roll(value, shift % value.shape[-1], value.ndim - 1)


def depth_edges(edges, cells):
    packed, group = None, 8
    for place, (velocity, stress_z, rigidity) in enumerate(cells):
        base = place * group
        lane = lane_of(velocity.shape)
        if packed is None:
            packed = jnp.zeros(velocity.shape, velocity.dtype)
        packed = jnp.where(
            lane < base,
            packed,
            jnp.where(
                lane < base + 4,
                turned(velocity, base + 2),
                jnp.where(lane < base + 6, turned(stress_z, base + 5), turned(rigidity, base + 7)),
            ),
        )
    size = packed.shape[0] * packed.shape[1]
    rows = packed.reshape(size, -1).T
    for place in range(len(cells)):
        edges[:, place * size : (place + 1) * size] = rows[place * group : (place + 1) * group]


def depth_sides(own, near, far, chunks):
    _, _, depth_even = parities()
    left = lax.select(depth_even, far, near)
    right = lax.select(depth_even, near, far)
    scale = courant * 0.5
    stress_left = left[4:5] + scale * left[6:7] * (own[2:3] - left[0:1])
    stress_right = right[5:6] + scale * right[7:8] * (right[3:4] - own[1:2])
    rows = jnp.concatenate(
        [right[2:3], left[1:2], stress_right, stress_left, jnp.zeros_like(left[:4])], axis=0
    )
    size = rows.shape[1] // chunks
    pieces = [rows[:, place * size : (place + 1) * size] for place in range(chunks)]
    pieces.append(jnp.zeros((size - 8 * chunks, size), rows.dtype))
    return jnp.concatenate(pieces, axis=0).T


def strike_edge(target, base, velocity, rigidity, stress_x, inner, sign):
    target[base : base + 16] = velocity
    target[base + 16 : base + 32] = rigidity
    target[base + 32 : base + 48] = stress_x + (sign * courant * 0.5) * rigidity * inner


def deal(total, core, own, surface):
    nodes = total.shape[0] // 5
    for place, index in enumerate((0, 2, 4)):
        own[surface, place * nodes : (place + 1) * nodes] = total[
            index * nodes : (index + 1) * nodes
        ]
    base = surface * 2 * nodes
    core[base : base + nodes] = total[nodes : 2 * nodes]
    core[base + nodes : base + 2 * nodes] = total[3 * nodes : 4 * nodes]


def first_kernel(*refs):
    (velocity, stress, rigidity, cone, history, kernel), rest = refs[:6], refs[6:11]
    core, own, later, lead, edges, speed, tension, rigid = refs[11:19]
    rest_held = refs[19:24]
    limits, past, matrix, slab_sems, part_sems, rest_sems = refs[24:]
    surfaces, rows, columns = kernel.shape
    nodes, ny, width = velocity.shape
    offsets = rows // nodes
    reach = (offsets - 1) // 2
    parts = columns // CHUNK_COLUMNS

    slab = [
        pltpu.make_async_copy(source, target, slab_sems.at[place])
        for place, (source, target) in enumerate(
            ((cone, limits), (velocity, speed), (rigidity, rigid), (stress, tension))
        )
    ]
    fetches = [
        (
            pltpu.make_async_copy(history.at[s], past.at[s], part_sems.at[0, s]),
            pltpu.make_async_copy(kernel.at[s], matrix.at[s], part_sems.at[1, s]),
        )
        for s in range(surfaces)
    ]
    others = [
        pltpu.make_async_copy(source, target, rest_sems.at[place])
        for place, (source, target) in enumerate(zip(rest, rest_held))
    ]
    for copy in (*slab, *fetches[0], *fetches[1], *others):
        copy.start()
    for copy in slab:
        copy.wait()

    cells = [slice(at, at + CHUNK) for at in range(0, nodes, CHUNK)]
    depth_edges(edges, [(speed[c], tension[1, c], rigid[c]) for c in cells])
    base = 4 * nodes
    strike_edge(core, base, speed[0], rigid[0], tension[0, 0], speed[1], 1.0)
    strike_edge(
        core,
        base + 48,
        speed[nodes - 1],
        rigid[nodes - 1],
        tension[0, nodes - 1],
        speed[nodes - 2],
        -1.0,
    )

    block = lax.axis_index(GX)
    blocks = cone.shape[3]
    lag = lax.div(lane_of((1, CHUNK_COLUMNS)), nodes)
    for surface in range(surfaces):
        for copy in fetches[surface]:
            copy.wait()
        total = None
        for part in range(parts):
            at = part * CHUNK_COLUMNS
            masked = []
            for index in range(offsets):
                target = jnp.clip(block + (index - reach), 0, blocks - 1)
                first = limits[surface, index, 0, target]
                last = limits[surface, index, 1, target]
                now = lag + at // nodes
                keep = jnp.where((now >= first) & (now < last), 1.0, 0.0).astype(jnp.bfloat16)
                masked.append(
                    matrix[surface, index * nodes : (index + 1) * nodes, at : at + CHUNK_COLUMNS]
                    * keep
                )
            kept = jnp.concatenate(masked, axis=0)
            now = past[surface, at : at + CHUNK_COLUMNS]
            if part:
                before = past[surface, at - nodes : at + CHUNK_COLUMNS - nodes]
            else:
                before = jnp.concatenate(
                    [jnp.zeros((nodes, width), now.dtype), now[: CHUNK_COLUMNS - nodes]], axis=0
                )
                lead[surface] = kept[:, :nodes]
            both = jnp.concatenate([now, before], axis=1)
            product = jnp.dot(kept, both, preferred_element_type=jnp.float32)
            total = total + product if part else product
        later[surface] = total[:, width:]
        deal(total[:, :width], core, own, surface)
    for copy in others:
        copy.wait()


def pinned(x):
    return pltpu.with_memory_space_constraint(x, pltpu.HBM)


def first_call(velocity, stress, rigidity, cone, history, kernel, *rest):
    surfaces, rows, columns = kernel.shape
    nodes, ny, width = velocity.shape
    f32 = jnp.float32
    return pl.pallas_call(
        first_kernel,
        in_specs=[pl.BlockSpec(memory_space=pltpu.HBM)] * (6 + len(rest)),
        out_specs=[pl.BlockSpec(memory_space=pltpu.VMEM)] * (8 + len(rest)),
        out_shape=[
            jax.ShapeDtypeStruct((4 * nodes + 96, width), f32),
            jax.ShapeDtypeStruct((surfaces, 3 * nodes, width), f32),
            jax.ShapeDtypeStruct((surfaces, rows, width), f32),
            jax.ShapeDtypeStruct((surfaces, rows, nodes), jnp.bfloat16),
            jax.ShapeDtypeStruct((8, nodes * ny), f32),
        ]
        + [jax.ShapeDtypeStruct(x.shape, x.dtype) for x in (velocity, stress, rigidity, *rest)],
        scratch_shapes=[
            pltpu.SMEM(cone.shape, jnp.int32),
            pltpu.VMEM(history.shape, history.dtype),
            pltpu.VMEM(kernel.shape, kernel.dtype),
            pltpu.SemaphoreType.DMA((4,)),
            pltpu.SemaphoreType.DMA((2, surfaces)),
            pltpu.SemaphoreType.DMA((len(rest),)),
        ],
        compiler_params=pltpu.CompilerParams(vmem_limit_bytes=FIRST_LIMIT),
    )(*(pinned(x) for x in (velocity, stress, rigidity, cone, history, kernel, *rest)))


def relay_kernel(received, own, far, near):
    even, chip_even, _ = parities()
    nodes = own.shape[1] // 3
    right, left = [], []
    for surface in range(2):
        base = surface * 2 * nodes
        from_left = received[base : base + nodes]
        from_right = received[base + nodes : base + 2 * nodes]
        nothing = jnp.zeros_like(from_left)
        left.append(own[surface, :nodes] + lax.select(even, nothing, from_left))
        right.append(own[surface, 2 * nodes :] + lax.select(even, from_right, nothing))
    left.append(received[4 * nodes : 4 * nodes + 48])
    right.append(received[4 * nodes + 48 :])
    base = 0
    for to_left, to_right in zip(left, right):
        size = to_left.shape[0]
        near[base : base + size] = lax.select(chip_even, to_right, to_left)
        far[base : base + size] = lax.select(chip_even, to_left, to_right)
        base += size
    far[base:] = jnp.zeros_like(far[base:])


def relay_call(received, own):
    nodes, width = own.shape[1] // 3, own.shape[2]
    rows = 2 * nodes + 48
    return pl.pallas_call(
        relay_kernel,
        out_shape=[
            jax.ShapeDtypeStruct((rows + SPARE, width), jnp.float32),
            jax.ShapeDtypeStruct((rows, width), jnp.float32),
        ],
        compiler_params=pltpu.CompilerParams(vmem_limit_bytes=4 * MIB),
    )(received, own)


def step_kernel(last, *refs):
    (velocity, stress, stress_y, rigidity, buoyancy, sigma_star, sigma_zero, friction) = refs[:8]
    (received, near, far, depth_own, depth_near, depth_far, own) = refs[8:15]
    refs = refs[15:]
    if last:
        results, held, sems = refs[:5], refs[5:10], refs[10]
        velocity_new, stress_new, stress_y_new, state_new, bounds = held
        traction = refs[11]
        copies = []

        def send(sources, targets):
            for source, target in zip(sources, targets):
                copies.append(pltpu.make_async_copy(source, target, sems.at[len(copies)]))
                copies[-1].start()

    else:
        later, lead = refs[:2]
        velocity_new, stress_new, stress_y_new, state_new, core, own_new, edges = refs[2:9]
        traction, newest = refs[9:]
    even, chip_even, _ = parities()
    nodes, ny, width = velocity.shape
    chunks = nodes // CHUNK
    fault = ny // 2 - 1
    scale = courant * 0.5

    for surface in range(2):
        base = surface * 2 * nodes
        mate = lax.select(
            even, received[base : base + nodes], received[base + nodes : base + 2 * nodes]
        )
        rows = slice(surface * nodes, (surface + 1) * nodes)
        traction[surface] = own[surface, nodes : 2 * nodes] + mate + near[rows] + far[rows]

    near_halo, far_halo = (x[2 * nodes : 2 * nodes + 48] for x in (near, far))
    left = lax.select(
        even, lax.select(chip_even, far_halo, near_halo), received[4 * nodes + 48 :]
    )
    right = lax.select(
        even, received[4 * nodes : 4 * nodes + 48], lax.select(chip_even, near_halo, far_halo)
    )
    stress_left = left[32:] + scale * left[16:32] * velocity[0]
    stress_right = right[32:] - scale * right[16:32] * velocity[nodes - 1]
    sides = depth_sides(depth_own[...], depth_near[...], depth_far[...], chunks)

    shape = (CHUNK, ny, width)
    sides = sides.reshape(shape)
    lane = lane_of(shape)
    level = lax.broadcasted_iota(jnp.int32, shape, 1)

    def beside(ref, at, before, after):
        up = ref[at + 1 : min(at + CHUNK + 1, nodes)]
        down = ref[max(at - 1, 0) : at + CHUNK - 1]
        if at + CHUNK == nodes:
            up = jnp.concatenate([up, after[None]], axis=0)
        if at == 0:
            down = jnp.concatenate([before[None], down], axis=0)
        return up, down

    def stresses(at):
        cells = slice(at, at + CHUNK)
        here, rigid = velocity[cells], rigidity[cells]
        up, down = beside(velocity, at, left[:16], right[:16])
        stress_x = stress[0, cells] + scale * rigid * (up - down)
        stress_new[0, cells] = stress_x

        place = 8 * (at // CHUNK)
        side = turned(sides, -(place + 1))
        after = jnp.where(lane == width - 1, side, turned(here, -1))
        before = jnp.where(lane == 0, side, turned(here, 1))
        stress_z = stress[1, cells] + scale * rigid * (after - before)
        stress_new[1, cells] = stress_z
        side = turned(sides, -(place + 3))
        after = jnp.where(lane == width - 1, side, turned(stress_z, -1))
        before = jnp.where(lane == 0, side, turned(stress_z, 1))
        spreading = 0.5 * (after - before)

        if last:
            faces = stress_y[cells][:, : ny - 1]
        else:
            faces = jnp.stack(
                [stress_y[pl.ds(at + r, ny - 1, stride=nodes), :] for r in range(CHUNK)]
            )
        trial = faces + courant * (0.5 * (rigid[:, 1:] + rigid[:, :-1])) * (
            here[:, 1:] - here[:, :-1]
        )
        slip_rate = here[:, fault + 1] - here[:, fault]
        zero = sigma_zero[cells]
        normal = zero + bimaterial * jnp.tanh(stress_x[:, fault + 1] - stress_x[:, fault])
        state = normal + (sigma_star[cells] - normal) * jnp.exp(
            -(jnp.abs(slip_rate) + slip_ref) * decay_rate
        )
        state_new[cells] = state
        strength = friction[cells] * state
        clipped = jnp.clip(trial[:, fault], -strength, strength)
        bottom = traction[0, cells] + impedance * here[:, 0]
        top = traction[1, cells] - impedance * here[:, ny - 1]
        above = jnp.concatenate([trial, top[:, None]], axis=1)
        above = jnp.where(level == fault, clipped[:, None], above)
        if last:
            bounds[0, cells] = bottom
            bounds[1, cells] = top
            for r in range(CHUNK):
                stress_y_new[pl.ds(at + r, ny - 1, stride=nodes), :] = above[r, : ny - 1]
        else:
            stress_y_new[cells] = above
        below = jnp.where(level == 0, bottom[:, None], pltpu.roll(above, 1, 1))
        return spreading + above - below

    def velocities(at, partial):
        cells = slice(at, at + CHUNK)
        up, down = beside(stress_new.at[0], at, stress_left, stress_right)
        moved = velocity[cells] + courant * buoyancy[cells] * (0.5 * (up - down) + partial)
        velocity_new[cells] = moved
        if not last:
            newest[0, cells] = moved[:, 0]
            newest[1, cells] = moved[:, ny - 1]

    partial = stresses(0)
    for at in range(CHUNK, nodes, CHUNK):
        following = stresses(at)
        velocities(at - CHUNK, partial)
        partial = following
        if last and at == nodes // 2:
            half = pl.ds(0, at)
            send(
                [stress_new.at[:, half], velocity_new.at[pl.ds(0, at - CHUNK)]],
                [results[1].at[:, half], results[0].at[pl.ds(0, at - CHUNK)]],
            )
    if last:
        half = pl.ds(nodes // 2, nodes // 2)
        send(
            [stress_new.at[:, half], stress_y_new, state_new, bounds],
            [results[1].at[:, half], results[2], results[3], results[4]],
        )
    velocities(nodes - CHUNK, partial)
    if last:
        half = pl.ds(nodes // 2 - CHUNK, nodes // 2 + CHUNK)
        send([velocity_new.at[half]], [results[0].at[half]])
        for copy in copies:
            copy.wait()
        return

    for surface in range(2):
        fresh = newest[surface].astype(jnp.bfloat16)
        total = later[surface] + jnp.dot(
            lead[surface], fresh, preferred_element_type=jnp.float32
        )
        deal(total, core, own_new, surface)
    strike_edge(
        core, 4 * nodes, velocity_new[0], rigidity[0], stress_new[0, 0], velocity_new[1], 1.0
    )
    strike_edge(
        core,
        4 * nodes + 48,
        velocity_new[nodes - 1],
        rigidity[nodes - 1],
        stress_new[0, nodes - 1],
        velocity_new[nodes - 2],
        -1.0,
    )
    cells = [slice(at, at + CHUNK) for at in range(0, nodes, CHUNK)]
    depth_edges(edges, [(velocity_new[c], stress_new[1, c], rigidity[c]) for c in cells])


def step_call(last, *args):
    nodes, ny, width = args[0].shape
    f32 = jnp.float32
    shapes = [(nodes, ny, width), (2, nodes, ny, width)]
    if last:
        shapes += [(nodes * (ny - 1), width), (nodes, width), (2, nodes, width)]
        scratch = [pltpu.VMEM(shape, f32) for shape in shapes]
        scratch += [pltpu.SemaphoreType.DMA((7,)), pltpu.VMEM((2, nodes, width), f32)]
        out_specs = [pl.BlockSpec(memory_space=pltpu.HBM)] * len(shapes)
    else:
        shapes += [
            (nodes, ny, width),
            (nodes, width),
            (4 * nodes + 96, width),
            (2, 3 * nodes, width),
            (8, nodes * ny),
        ]
        scratch = [pltpu.VMEM((2, nodes, width), f32)] * 2
        out_specs = [pl.BlockSpec(memory_space=pltpu.VMEM)] * len(shapes)
    return pl.pallas_call(
        functools.partial(step_kernel, last),
        out_shape=[jax.ShapeDtypeStruct(shape, f32) for shape in shapes],
        out_specs=out_specs,
        scratch_shapes=scratch,
        compiler_params=pltpu.CompilerParams(vmem_limit_bytes=16 * MIB),
    )(*args)


def depth_exchange(edges):
    far = lax.ppermute(edges, GZ, swap_pairs(GZ, 1, 1))
    near = lax.ppermute(edges, GZ, swap_pairs(GZ, 1, 0))
    return near, far


def strike_exchange(core, own):
    received = lax.ppermute(core, GX, swap_pairs(GX, 1, 0))
    far, near = relay_call(received, own)
    far = lax.ppermute(far, GX, swap_pairs(GX, 2, 2))
    near = lax.ppermute(near, GX, swap_pairs(GX, 2, 0))
    return received, near, far


def local(
    velocity,
    stress_xz,
    stress_y,
    rigidity,
    buoyancy,
    sigma_star,
    sigma_zero,
    friction,
    history,
    kernel,
    cone,
):
    surfaces, lags, nodes, width = history.shape
    faces = stress_y.shape[1]
    past = history.reshape(surfaces, lags * nodes, width)
    matrix = kernel.reshape(surfaces, -1, kernel.shape[3])
    turned_cone = jnp.transpose(cone, (0, 2, 3, 1))
    face_rows = jnp.transpose(stress_y, (1, 0, 2)).reshape(faces * nodes, width)
    core, own, later, lead, edges, velocity, stress_xz, rigidity, *rest = first_call(
        velocity,
        stress_xz,
        rigidity,
        turned_cone,
        past,
        matrix,
        face_rows,
        buoyancy,
        sigma_star,
        sigma_zero,
        friction,
    )
    face_rows, buoyancy, sigma_star, sigma_zero, friction = rest
    moved = (*strike_exchange(core, own), edges, *depth_exchange(edges))
    velocity, stress_xz, stress_y, state, core, own, edges = step_call(
        False,
        velocity,
        stress_xz,
        face_rows,
        rigidity,
        buoyancy,
        sigma_star,
        sigma_zero,
        friction,
        *moved,
        own,
        later,
        lead,
    )
    moved = (*strike_exchange(core, own), edges, *depth_exchange(edges))
    velocity, stress_xz, face_rows, state, bounds = step_call(
        True,
        velocity,
        stress_xz,
        stress_y,
        rigidity,
        buoyancy,
        state,
        sigma_zero,
        friction,
        *moved,
        own,
    )
    stress_y = jnp.transpose(face_rows.reshape(faces, nodes, width), (1, 0, 2))
    return velocity, stress_xz, stress_y, state, bounds


def solution(mesh):
    in_specs = (
        P("gx", None, "gz"),
        P(None, "gx", None, "gz"),
        P("gx", None, "gz"),
        P("gx", None, "gz"),
        P("gx", None, "gz"),
        P("gx", "gz"),
        P("gx", "gz"),
        P("gx", "gz"),
        P(None, None, "gx", "gz"),
        P(),
        P(),
    )
    out_specs = (
        P("gx", None, "gz"),
        P(None, "gx", None, "gz"),
        P("gx", None, "gz"),
        P("gx", "gz"),
        P(None, "gx", "gz"),
    )
    return jax.shard_map(
        local, mesh=mesh, in_specs=in_specs, out_specs=tuple(out_specs), check_vma=False
    )
```

```python
import functools

import jax
import jax.numpy as jnp
from jax import lax
from jax.experimental import pallas as pl
from jax.experimental.pallas import tpu as pltpu
from jax.sharding import PartitionSpec as P

courant = 0.25
bimaterial = 0.5
slip_ref = 0.2
decay_rate = 0.5
impedance = 0.5

GX, GZ = "gx", "gz"
CHUNK = 8
CHUNK_COLUMNS = 1024
SPARE = 32
MIB = 2**20
FIRST_LIMIT = 12 * MIB


def swap_pairs(axis, distance, phase):
    size, pairs = lax.axis_size(axis), []
    for i in range(size):
        partner = i + distance if (i - phase) % (2 * distance) < distance else i - distance
        if 0 <= partner < size:
            pairs.append((i, partner))
    return pairs


def onward_pairs(axis):
    size, pairs = lax.axis_size(axis), []
    for i in range(size):
        partner = i + 2 if i % 2 == 0 else i - 2
        if 0 <= partner < size:
            pairs.append((i, partner))
    return pairs


def parities():
    block = lax.axis_index(GX)
    even = lax.rem(block, 2) == 0
    chip_even = lax.rem(lax.div(block, 2), 2) == 0
    depth_even = lax.rem(lax.axis_index(GZ), 2) == 0
    return even, chip_even, depth_even


def lane_of(shape):
    return lax.broadcasted_iota(jnp.int32, shape, len(shape) - 1)


def turned(value, shift):
    return pltpu.roll(value, shift % value.shape[-1], value.ndim - 1)


def depth_edges(edges, edges_sent, cells):
    packed, group = None, 8
    for place, (velocity, stress_z, rigidity) in enumerate(cells):
        base = place * group
        lane = lane_of(velocity.shape)
        if packed is None:
            packed = jnp.zeros(velocity.shape, velocity.dtype)
        packed = jnp.where(
            lane < base,
            packed,
            jnp.where(
                lane < base + 4,
                turned(velocity, base + 2),
                jnp.where(lane < base + 6, turned(stress_z, base + 5), turned(rigidity, base + 7)),
            ),
        )
    size = packed.shape[0] * packed.shape[1]
    rows = packed.reshape(size, -1).T
    for place in range(len(cells)):
        edges[:, place * size : (place + 1) * size] = rows[place * group : (place + 1) * group]
    edges_sent[...] = rows[: edges_sent.shape[0]].astype(edges_sent.dtype)


def depth_sides(own, near, far, chunks):
    _, _, depth_even = parities()
    near, far = (
        jnp.concatenate([x[at : at + 8] for at in range(0, x.shape[0], 8)], axis=1)
        for x in (near.astype(jnp.float32), far.astype(jnp.float32))
    )
    left = lax.select(depth_even, far, near)
    right = lax.select(depth_even, near, far)
    scale = courant * 0.5
    stress_left = left[4:5] + scale * left[6:7] * (own[2:3] - left[0:1])
    stress_right = right[5:6] + scale * right[7:8] * (right[3:4] - own[1:2])
    rows = jnp.concatenate(
        [right[2:3], left[1:2], stress_right, stress_left, jnp.zeros_like(left[:4])], axis=0
    )
    size = rows.shape[1] // chunks
    pieces = [rows[:, place * size : (place + 1) * size] for place in range(chunks)]
    pieces.append(jnp.zeros((size - 8 * chunks, size), rows.dtype))
    return jnp.concatenate(pieces, axis=0).T


def strike_edge(target, base, velocity, rigidity, stress_x, inner, sign):
    target[base : base + 16] = velocity
    target[base + 16 : base + 32] = rigidity
    target[base + 32 : base + 48] = stress_x + (sign * courant * 0.5) * rigidity * inner


def deal(total, core, own, surface):
    nodes = total.shape[0] // 5
    for place, index in enumerate((0, 2, 4)):
        own[surface, place * nodes : (place + 1) * nodes] = total[
            index * nodes : (index + 1) * nodes
        ]
    base = surface * 2 * nodes
    core[base : base + nodes] = total[nodes : 2 * nodes]
    core[base + nodes : base + 2 * nodes] = total[3 * nodes : 4 * nodes]


def first_kernel(*refs):
    (velocity, stress, rigidity, cone, history, kernel), rest = refs[:6], refs[6:11]
    core, own, later, lead, edges, edges_sent, speed, tension, rigid = refs[11:20]
    rest_held = refs[20:25]
    limits, past, matrix, slab_sems, part_sems, rest_sems = refs[25:]
    surfaces, rows, columns = kernel.shape
    nodes, ny, width = velocity.shape
    offsets = rows // nodes
    reach = (offsets - 1) // 2
    parts = columns // CHUNK_COLUMNS

    slab = [
        pltpu.make_async_copy(source, target, slab_sems.at[place])
        for place, (source, target) in enumerate(
            ((cone, limits), (velocity, speed), (rigidity, rigid), (stress, tension))
        )
    ]
    fetches = [
        (
            pltpu.make_async_copy(history.at[s], past.at[s], part_sems.at[0, s]),
            pltpu.make_async_copy(kernel.at[s], matrix.at[s], part_sems.at[1, s]),
        )
        for s in range(surfaces)
    ]
    others = [
        pltpu.make_async_copy(source, target, rest_sems.at[place])
        for place, (source, target) in enumerate(zip(rest, rest_held))
    ]
    for copy in (slab[0], *fetches[0]):
        copy.start()
    slab[0].wait()
    for copy in (*fetches[1], *slab[1:]):
        copy.start()

    block = lax.axis_index(GX)
    blocks = cone.shape[3]
    lag = lax.div(lane_of((1, CHUNK_COLUMNS)), nodes)
    for surface in range(surfaces):
        for copy in fetches[surface]:
            copy.wait()
        if surface == 0:
            for copy in others:
                copy.start()
        total = None
        for part in range(parts):
            at = part * CHUNK_COLUMNS
            masked = []
            for index in range(offsets):
                target = jnp.clip(block + (index - reach), 0, blocks - 1)
                first = limits[surface, index, 0, target]
                last = limits[surface, index, 1, target]
                now = lag + at // nodes
                keep = jnp.where((now >= first) & (now < last), 1.0, 0.0).astype(jnp.bfloat16)
                masked.append(
                    matrix[surface, index * nodes : (index + 1) * nodes, at : at + CHUNK_COLUMNS]
                    * keep
                )
            kept = jnp.concatenate(masked, axis=0)
            now = past[surface, at : at + CHUNK_COLUMNS]
            if part:
                before = past[surface, at - nodes : at + CHUNK_COLUMNS - nodes]
            else:
                before = jnp.concatenate(
                    [jnp.zeros((nodes, width), now.dtype), now[: CHUNK_COLUMNS - nodes]], axis=0
                )
                lead[surface] = kept[:, :nodes]
            both = jnp.concatenate([now, before], axis=1)
            product = jnp.dot(kept, both, preferred_element_type=jnp.float32)
            total = total + product if part else product
        later[surface] = total[:, width:]
        deal(total[:, :width], core, own, surface)
        if surface == 0:
            for copy in slab[1:]:
                copy.wait()
            cells = [slice(at, at + CHUNK) for at in range(0, nodes, CHUNK)]
            depth_edges(edges, edges_sent, [(speed[c], tension[1, c], rigid[c]) for c in cells])
            base = 4 * nodes
            strike_edge(core, base, speed[0], rigid[0], tension[0, 0], speed[1], 1.0)
            strike_edge(
                core,
                base + 48,
                speed[nodes - 1],
                rigid[nodes - 1],
                tension[0, nodes - 1],
                speed[nodes - 2],
                -1.0,
            )
    for copy in others:
        copy.wait()


def pinned(x):
    return pltpu.with_memory_space_constraint(x, pltpu.HBM)


def first_call(velocity, stress, rigidity, cone, history, kernel, *rest):
    surfaces, rows, columns = kernel.shape
    nodes, ny, width = velocity.shape
    f32 = jnp.float32
    return pl.pallas_call(
        first_kernel,
        in_specs=[pl.BlockSpec(memory_space=pltpu.HBM)] * (6 + len(rest)),
        out_specs=[pl.BlockSpec(memory_space=pltpu.VMEM)] * (9 + len(rest)),
        out_shape=[
            jax.ShapeDtypeStruct((4 * nodes + 96, width), f32),
            jax.ShapeDtypeStruct((surfaces, 3 * nodes, width), f32),
            jax.ShapeDtypeStruct((surfaces, rows, width), f32),
            jax.ShapeDtypeStruct((surfaces, rows, nodes), jnp.bfloat16),
            jax.ShapeDtypeStruct((8, nodes * ny), f32),
            jax.ShapeDtypeStruct((nodes, width), jnp.bfloat16),
        ]
        + [jax.ShapeDtypeStruct(x.shape, x.dtype) for x in (velocity, stress, rigidity, *rest)],
        scratch_shapes=[
            pltpu.SMEM(cone.shape, jnp.int32),
            pltpu.VMEM(history.shape, history.dtype),
            pltpu.VMEM(kernel.shape, kernel.dtype),
            pltpu.SemaphoreType.DMA((4,)),
            pltpu.SemaphoreType.DMA((2, surfaces)),
            pltpu.SemaphoreType.DMA((len(rest),)),
        ],
        compiler_params=pltpu.CompilerParams(vmem_limit_bytes=FIRST_LIMIT),
    )(*(pinned(x) for x in (velocity, stress, rigidity, cone, history, kernel, *rest)))


def packed_into(target, parts):
    base, powers = 0, []
    for part in parts:
        size = part.shape[0]
        most = jnp.max(jnp.abs(part), axis=0, keepdims=True)
        power = jnp.ceil(jnp.log2(jnp.maximum(most, 2.0**-100)))
        powers.append(power)
        target[base : base + size] = jnp.round(part * jnp.exp2(14.0 - power)).astype(jnp.int16)
        base += size
    powers.append(jnp.zeros((16 - len(powers), powers[0].shape[1]), jnp.float32))
    target[base : base + 16] = jnp.concatenate(powers, axis=0).astype(jnp.int16)
    if target.shape[0] > base + 16:
        target[base + 16 :] = jnp.zeros_like(target[base + 16 :])


def unpacked(source, nodes):
    sizes = (nodes, nodes, 16, 16, 16)
    base, parts = 0, []
    last = sum(sizes)
    scales = jnp.exp2(source[last : last + 16].astype(jnp.float32) - 14.0)
    for place, size in enumerate(sizes):
        part = source[base : base + size].astype(jnp.float32)
        parts.append(part * scales[place : place + 1])
        base += size
    return parts


def relay_kernel(near, received, own, *refs):
    target = refs[-1]
    even, chip_even, _ = parities()
    to_right = chip_even if near else jnp.logical_not(chip_even)
    nodes = own.shape[1] // 3
    parts = []
    for surface in range(2):
        base = surface * 2 * nodes
        from_left = received[base : base + nodes]
        from_right = received[base + nodes : base + 2 * nodes]
        nothing = jnp.zeros_like(from_left)
        left = own[surface, :nodes] + lax.select(even, nothing, from_left)
        right = own[surface, 2 * nodes :] + lax.select(even, from_right, nothing)
        parts.append(lax.select(to_right, right, left))
    base = 4 * nodes
    halo = lax.select(to_right, received[base + 48 :], received[base : base + 48])
    packed_into(target, parts + [halo[at : at + 16] for at in (0, 16, 32)])


def relay_call(near, received, own, *after):
    nodes, width = own.shape[1] // 3, own.shape[2]
    rows = 2 * nodes + 64 + (0 if near else SPARE)
    return pl.pallas_call(
        functools.partial(relay_kernel, near),
        out_shape=jax.ShapeDtypeStruct((rows, width), jnp.int16),
        compiler_params=pltpu.CompilerParams(vmem_limit_bytes=4 * MIB),
    )(received, own, *after)


def step_kernel(last, *refs):
    (velocity, stress, stress_y, rigidity, buoyancy, sigma_star, sigma_zero, friction) = refs[:8]
    (received, near, far, depth_own, depth_near, depth_far, own) = refs[8:15]
    refs = refs[15:]
    if last:
        results, held, sems = refs[:5], refs[5:10], refs[10]
        velocity_new, stress_new, stress_y_new, state_new, bounds = held
        traction = refs[11]
        copies = []

        def send(sources, targets):
            for source, target in zip(sources, targets):
                copies.append(pltpu.make_async_copy(source, target, sems.at[len(copies)]))
                copies[-1].start()

    else:
        later, lead = refs[:2]
        velocity_new, stress_new, stress_y_new, state_new, core, own_new, edges = refs[2:9]
        edges_sent, traction, newest = refs[9:]
    even, chip_even, _ = parities()
    nodes, ny, width = velocity.shape
    chunks = nodes // CHUNK
    fault = ny // 2 - 1
    scale = courant * 0.5

    near_parts, far_parts = unpacked(near, nodes), unpacked(far, nodes)
    for surface in range(2):
        base = surface * 2 * nodes
        mate = lax.select(
            even, received[base : base + nodes], received[base + nodes : base + 2 * nodes]
        )
        rows = slice(surface * nodes, (surface + 1) * nodes)
        traction[surface] = (
            own[surface, nodes : 2 * nodes] + mate + (near_parts[surface] + far_parts[surface])
        )

    near_halo, far_halo = (jnp.concatenate(x[2:], axis=0) for x in (near_parts, far_parts))
    left = lax.select(
        even, lax.select(chip_even, far_halo, near_halo), received[4 * nodes + 48 :]
    )
    right = lax.select(
        even, received[4 * nodes : 4 * nodes + 48], lax.select(chip_even, near_halo, far_halo)
    )
    stress_left = left[32:] + scale * left[16:32] * velocity[0]
    stress_right = right[32:] - scale * right[16:32] * velocity[nodes - 1]
    sides = depth_sides(depth_own[...], depth_near[...], depth_far[...], chunks)

    shape = (CHUNK, ny, width)
    sides = sides.reshape(shape)
    lane = lane_of(shape)
    level = lax.broadcasted_iota(jnp.int32, shape, 1)

    def beside(ref, at, before, after):
        up = ref[at + 1 : min(at + CHUNK + 1, nodes)]
        down = ref[max(at - 1, 0) : at + CHUNK - 1]
        if at + CHUNK == nodes:
            up = jnp.concatenate([up, after[None]], axis=0)
        if at == 0:
            down = jnp.concatenate([before[None], down], axis=0)
        return up, down

    def stresses(at):
        cells = slice(at, at + CHUNK)
        here, rigid = velocity[cells], rigidity[cells]
        up, down = beside(velocity, at, left[:16], right[:16])
        stress_x = stress[0, cells] + scale * rigid * (up - down)
        stress_new[0, cells] = stress_x

        place = 8 * (at // CHUNK)
        side = turned(sides, -(place + 1))
        after = jnp.where(lane == width - 1, side, turned(here, -1))
        before = jnp.where(lane == 0, side, turned(here, 1))
        stress_z = stress[1, cells] + scale * rigid * (after - before)
        stress_new[1, cells] = stress_z
        side = turned(sides, -(place + 3))
        after = jnp.where(lane == width - 1, side, turned(stress_z, -1))
        before = jnp.where(lane == 0, side, turned(stress_z, 1))
        spreading = 0.5 * (after - before)

        if last:
            faces = stress_y[cells][:, : ny - 1]
        else:
            faces = jnp.stack(
                [stress_y[pl.ds(at + r, ny - 1, stride=nodes), :] for r in range(CHUNK)]
            )
        trial = faces + courant * (0.5 * (rigid[:, 1:] + rigid[:, :-1])) * (
            here[:, 1:] - here[:, :-1]
        )
        slip_rate = here[:, fault + 1] - here[:, fault]
        zero = sigma_zero[cells]
        normal = zero + bimaterial * jnp.tanh(stress_x[:, fault + 1] - stress_x[:, fault])
        state = normal + (sigma_star[cells] - normal) * jnp.exp(
            -(jnp.abs(slip_rate) + slip_ref) * decay_rate
        )
        state_new[cells] = state
        strength = friction[cells] * state
        clipped = jnp.clip(trial[:, fault], -strength, strength)
        bottom = traction[0, cells] + impedance * here[:, 0]
        top = traction[1, cells] - impedance * here[:, ny - 1]
        above = jnp.concatenate([trial, top[:, None]], axis=1)
        above = jnp.where(level == fault, clipped[:, None], above)
        if last:
            bounds[0, cells] = bottom
            bounds[1, cells] = top
            for r in range(CHUNK):
                stress_y_new[pl.ds(at + r, ny - 1, stride=nodes), :] = above[r, : ny - 1]
        else:
            stress_y_new[cells] = above
        below = jnp.where(level == 0, bottom[:, None], pltpu.roll(above, 1, 1))
        return spreading + above - below

    def velocities(at, partial):
        cells = slice(at, at + CHUNK)
        up, down = beside(stress_new.at[0], at, stress_left, stress_right)
        moved = velocity[cells] + courant * buoyancy[cells] * (0.5 * (up - down) + partial)
        velocity_new[cells] = moved
        if not last:
            newest[0, cells] = moved[:, 0]
            newest[1, cells] = moved[:, ny - 1]

    partial = stresses(0)
    for at in range(CHUNK, nodes, CHUNK):
        following = stresses(at)
        velocities(at - CHUNK, partial)
        partial = following
        if last and at == nodes // 2:
            half = pl.ds(0, at)
            send(
                [stress_new.at[:, half], velocity_new.at[pl.ds(0, at - CHUNK)]],
                [results[1].at[:, half], results[0].at[pl.ds(0, at - CHUNK)]],
            )
    if last:
        half = pl.ds(nodes // 2, nodes // 2)
        send(
            [stress_new.at[:, half], stress_y_new, state_new, bounds],
            [results[1].at[:, half], results[2], results[3], results[4]],
        )
    velocities(nodes - CHUNK, partial)
    if last:
        half = pl.ds(nodes // 2 - CHUNK, nodes // 2 + CHUNK)
        send([velocity_new.at[half]], [results[0].at[half]])
        for copy in copies:
            copy.wait()
        return

    for surface in range(2):
        fresh = newest[surface].astype(jnp.bfloat16)
        total = later[surface] + jnp.dot(
            lead[surface], fresh, preferred_element_type=jnp.float32
        )
        deal(total, core, own_new, surface)
    strike_edge(
        core, 4 * nodes, velocity_new[0], rigidity[0], stress_new[0, 0], velocity_new[1], 1.0
    )
    strike_edge(
        core,
        4 * nodes + 48,
        velocity_new[nodes - 1],
        rigidity[nodes - 1],
        stress_new[0, nodes - 1],
        velocity_new[nodes - 2],
        -1.0,
    )
    cells = [slice(at, at + CHUNK) for at in range(0, nodes, CHUNK)]
    depth_edges(edges, edges_sent, [(velocity_new[c], stress_new[1, c], rigidity[c]) for c in cells])


def step_call(last, *args):
    nodes, ny, width = args[0].shape
    f32 = jnp.float32
    shapes = [(nodes, ny, width), (2, nodes, ny, width)]
    if last:
        shapes += [(nodes * (ny - 1), width), (nodes, width), (2, nodes, width)]
        scratch = [pltpu.VMEM(shape, f32) for shape in shapes]
        scratch += [pltpu.SemaphoreType.DMA((7,)), pltpu.VMEM((2, nodes, width), f32)]
        out_specs = [pl.BlockSpec(memory_space=pltpu.HBM)] * len(shapes)
    else:
        shapes += [
            (nodes, ny, width),
            (nodes, width),
            (4 * nodes + 96, width),
            (2, 3 * nodes, width),
            (8, nodes * ny),
        ]
        scratch = [pltpu.VMEM((2, nodes, width), f32)] * 2
        out_specs = [pl.BlockSpec(memory_space=pltpu.VMEM)] * (len(shapes) + 1)
    out_shape = [jax.ShapeDtypeStruct(shape, f32) for shape in shapes]
    if not last:
        out_shape.append(jax.ShapeDtypeStruct((nodes, width), jnp.bfloat16))
    return pl.pallas_call(
        functools.partial(step_kernel, last),
        out_shape=out_shape,
        out_specs=out_specs,
        scratch_shapes=scratch,
        compiler_params=pltpu.CompilerParams(vmem_limit_bytes=16 * MIB),
    )(*args)


def exchange(core, own, edges, edges_sent):
    received = lax.ppermute(core, GX, swap_pairs(GX, 1, 0))
    depth_near = lax.ppermute(edges_sent, GZ, swap_pairs(GZ, 1, 0))
    far = lax.ppermute(relay_call(False, received, own), GX, swap_pairs(GX, 2, 2))
    near = relay_call(True, received, own, depth_near)
    near = lax.ppermute(near, GX, swap_pairs(GX, 2, 0))
    depth_far = lax.ppermute(depth_near, GZ, onward_pairs(GZ))
    return received, near, far, edges, depth_near, depth_far


def local(
    velocity,
    stress_xz,
    stress_y,
    rigidity,
    buoyancy,
    sigma_star,
    sigma_zero,
    friction,
    history,
    kernel,
    cone,
):
    surfaces, lags, nodes, width = history.shape
    faces = stress_y.shape[1]
    past = history.reshape(surfaces, lags * nodes, width)
    matrix = kernel.reshape(surfaces, -1, kernel.shape[3])
    turned_cone = jnp.transpose(cone, (0, 2, 3, 1))
    face_rows = jnp.transpose(stress_y, (1, 0, 2)).reshape(faces * nodes, width)
    core, own, later, lead, edges, sent, velocity, stress_xz, rigidity, *rest = first_call(
        velocity,
        stress_xz,
        rigidity,
        turned_cone,
        past,
        matrix,
        face_rows,
        buoyancy,
        sigma_star,
        sigma_zero,
        friction,
    )
    face_rows, buoyancy, sigma_star, sigma_zero, friction = rest
    moved = exchange(core, own, edges, sent)
    velocity, stress_xz, stress_y, state, core, own, edges, sent = step_call(
        False,
        velocity,
        stress_xz,
        face_rows,
        rigidity,
        buoyancy,
        sigma_star,
        sigma_zero,
        friction,
        *moved,
        own,
        later,
        lead,
    )
    moved = exchange(core, own, edges, sent)
    velocity, stress_xz, face_rows, state, bounds = step_call(
        True,
        velocity,
        stress_xz,
        stress_y,
        rigidity,
        buoyancy,
        state,
        sigma_zero,
        friction,
        *moved,
        own,
    )
    stress_y = jnp.transpose(face_rows.reshape(faces, nodes, width), (1, 0, 2))
    return velocity, stress_xz, stress_y, state, bounds


def solution(mesh):
    in_specs = (
        P("gx", None, "gz"),
        P(None, "gx", None, "gz"),
        P("gx", None, "gz"),
        P("gx", None, "gz"),
        P("gx", None, "gz"),
        P("gx", "gz"),
        P("gx", "gz"),
        P("gx", "gz"),
        P(None, None, "gx", "gz"),
        P(),
        P(),
    )
    out_specs = (
        P("gx", None, "gz"),
        P(None, "gx", None, "gz"),
        P("gx", None, "gz"),
        P("gx", "gz"),
        P(None, "gx", "gz"),
    )
    return jax.shard_map(
        local, mesh=mesh, in_specs=in_specs, out_specs=tuple(out_specs), check_vma=False
    )
```

```python
import functools

import jax
import jax.numpy as jnp
from jax import lax
from jax.experimental import pallas as pl
from jax.experimental.pallas import tpu as pltpu
from jax.sharding import PartitionSpec as P

courant = 0.25
bimaterial = 0.5
slip_ref = 0.2
decay_rate = 0.5
impedance = 0.5

GX, GZ = "gx", "gz"
CHUNK = 8
CHUNK_COLUMNS = 1024
SPARE = 32
MIB = 2**20
FIRST_LIMIT = 12 * MIB


def swap_pairs(axis, distance, phase):
    size, pairs = lax.axis_size(axis), []
    for i in range(size):
        partner = i + distance if (i - phase) % (2 * distance) < distance else i - distance
        if 0 <= partner < size:
            pairs.append((i, partner))
    return pairs


def onward_pairs(axis):
    size, pairs = lax.axis_size(axis), []
    for i in range(size):
        partner = i + 2 if i % 2 == 0 else i - 2
        if 0 <= partner < size:
            pairs.append((i, partner))
    return pairs


def parities():
    block = lax.axis_index(GX)
    even = lax.rem(block, 2) == 0
    chip_even = lax.rem(lax.div(block, 2), 2) == 0
    depth_even = lax.rem(lax.axis_index(GZ), 2) == 0
    return even, chip_even, depth_even


def lane_of(shape):
    return lax.broadcasted_iota(jnp.int32, shape, len(shape) - 1)


def turned(value, shift):
    return pltpu.roll(value, shift % value.shape[-1], value.ndim - 1)


def depth_edges(edges, edges_sent, cells):
    packed, group = None, 8
    for place, (velocity, stress_z, rigidity) in enumerate(cells):
        base = place * group
        lane = lane_of(velocity.shape)
        if packed is None:
            packed = jnp.zeros(velocity.shape, velocity.dtype)
        packed = jnp.where(
            lane < base,
            packed,
            jnp.where(
                lane < base + 4,
                turned(velocity, base + 2),
                jnp.where(lane < base + 6, turned(stress_z, base + 5), turned(rigidity, base + 7)),
            ),
        )
    size = packed.shape[0] * packed.shape[1]
    rows = packed.reshape(size, -1).T
    for place in range(len(cells)):
        edges[:, place * size : (place + 1) * size] = rows[place * group : (place + 1) * group]
    edges_sent[...] = rows[: edges_sent.shape[0]].astype(edges_sent.dtype)


def depth_sides(own, near, far, chunks):
    _, _, depth_even = parities()
    near, far = (
        jnp.concatenate([x[at : at + 8] for at in range(0, x.shape[0], 8)], axis=1)
        for x in (near.astype(jnp.float32), far.astype(jnp.float32))
    )
    left = lax.select(depth_even, far, near)
    right = lax.select(depth_even, near, far)
    scale = courant * 0.5
    stress_left = left[4:5] + scale * left[6:7] * (own[2:3] - left[0:1])
    stress_right = right[5:6] + scale * right[7:8] * (right[3:4] - own[1:2])
    first = -scale * own[7:8] * left[1:2]
    last = scale * own[6:7] * right[2:3]
    nothing = jnp.zeros_like(first)
    rows = [0.5 * last, 0.5 * stress_right, -0.5 * stress_left, -0.5 * first]
    rows = jnp.concatenate([*rows, last, first, nothing, nothing], axis=0)
    size = rows.shape[1] // chunks
    pieces = [rows[:, place * size : (place + 1) * size] for place in range(chunks)]
    pieces.append(jnp.zeros((size - 8 * chunks, size), rows.dtype))
    return jnp.concatenate(pieces, axis=0).T


def strike_edge(target, base, velocity, rigidity, stress_x, inner, sign):
    target[base : base + 16] = velocity
    target[base + 16 : base + 32] = rigidity
    target[base + 32 : base + 48] = stress_x + (sign * courant * 0.5) * rigidity * inner


def deal(total, core, own, surface):
    nodes = total.shape[0] // 5
    for place, index in enumerate((0, 2, 4)):
        own[surface, place * nodes : (place + 1) * nodes] = total[
            index * nodes : (index + 1) * nodes
        ]
    base = surface * 2 * nodes
    core[base : base + nodes] = total[nodes : 2 * nodes]
    core[base + nodes : base + 2 * nodes] = total[3 * nodes : 4 * nodes]


def first_kernel(*refs):
    (velocity, stress, rigidity, cone, history, kernel), rest = refs[:6], refs[6:11]
    core, own, later, lead, edges, edges_sent, speed, tension, rigid = refs[11:20]
    rest_held = refs[20:25]
    limits, past, matrix, slab_sems, part_sems, rest_sems = refs[25:]
    surfaces, rows, columns = kernel.shape
    nodes, ny, width = velocity.shape
    offsets = rows // nodes
    reach = (offsets - 1) // 2
    parts = columns // CHUNK_COLUMNS

    slab = [
        pltpu.make_async_copy(source, target, slab_sems.at[place])
        for place, (source, target) in enumerate(
            ((cone, limits), (velocity, speed), (rigidity, rigid), (stress, tension))
        )
    ]
    fetches = [
        (
            pltpu.make_async_copy(history.at[s], past.at[s], part_sems.at[0, s]),
            pltpu.make_async_copy(kernel.at[s], matrix.at[s], part_sems.at[1, s]),
        )
        for s in range(surfaces)
    ]
    others = [
        pltpu.make_async_copy(source, target.at[pl.ds(0, source.shape[0])], rest_sems.at[place])
        for place, (source, target) in enumerate(zip(rest, rest_held))
    ]
    for copy in (slab[0], *fetches[0]):
        copy.start()
    slab[0].wait()
    for copy in (*fetches[1], *slab[1:]):
        copy.start()

    block = lax.axis_index(GX)
    blocks = cone.shape[3]
    lag = lax.div(lane_of((1, CHUNK_COLUMNS)), nodes)
    for surface in range(surfaces):
        for copy in fetches[surface]:
            copy.wait()
        if surface == 0:
            for copy in others:
                copy.start()
        else:
            for copy in slab[1:]:
                copy.wait()
            cells = [slice(at, at + CHUNK) for at in range(0, nodes, CHUNK)]
            depth_edges(edges, edges_sent, [(speed[c], tension[1, c], rigid[c]) for c in cells])
            base = 4 * nodes
            strike_edge(core, base, speed[0], rigid[0], tension[0, 0], speed[1], 1.0)
            strike_edge(
                core,
                base + 48,
                speed[nodes - 1],
                rigid[nodes - 1],
                tension[0, nodes - 1],
                speed[nodes - 2],
                -1.0,
            )
        total = None
        for part in range(parts):
            at = part * CHUNK_COLUMNS
            masked = []
            for index in range(offsets):
                target = jnp.clip(block + (index - reach), 0, blocks - 1)
                first = limits[surface, index, 0, target]
                last = limits[surface, index, 1, target]
                now = lag + at // nodes
                keep = jnp.where((now >= first) & (now < last), 1.0, 0.0).astype(jnp.bfloat16)
                masked.append(
                    matrix[surface, index * nodes : (index + 1) * nodes, at : at + CHUNK_COLUMNS]
                    * keep
                )
            kept = jnp.concatenate(masked, axis=0)
            now = past[surface, at : at + CHUNK_COLUMNS]
            if part:
                before = past[surface, at - nodes : at + CHUNK_COLUMNS - nodes]
            else:
                before = jnp.concatenate(
                    [jnp.zeros((nodes, width), now.dtype), now[: CHUNK_COLUMNS - nodes]], axis=0
                )
                lead[surface] = kept[:, :nodes]
            both = jnp.concatenate([now, before], axis=1)
            product = jnp.dot(kept, both, preferred_element_type=jnp.float32)
            total = total + product if part else product
        later[surface] = total[:, width:]
        deal(total[:, :width], core, own, surface)
    for copy in others:
        copy.wait()


def pinned(x):
    return pltpu.with_memory_space_constraint(x, pltpu.HBM)


def first_call(velocity, stress, rigidity, cone, history, kernel, *rest):
    surfaces, rows, columns = kernel.shape
    nodes, ny, width = velocity.shape
    f32 = jnp.float32
    return pl.pallas_call(
        first_kernel,
        in_specs=[pl.BlockSpec(memory_space=pltpu.HBM)] * (6 + len(rest)),
        out_specs=[pl.BlockSpec(memory_space=pltpu.VMEM)] * (9 + len(rest)),
        out_shape=[
            jax.ShapeDtypeStruct((4 * nodes + 96, width), f32),
            jax.ShapeDtypeStruct((surfaces, 3 * nodes, width), f32),
            jax.ShapeDtypeStruct((surfaces, rows, width), f32),
            jax.ShapeDtypeStruct((surfaces, rows, nodes), jnp.bfloat16),
            jax.ShapeDtypeStruct((8, nodes * ny), f32),
            jax.ShapeDtypeStruct((nodes, width), jnp.bfloat16),
        ]
        + [
            jax.ShapeDtypeStruct(shape, f32)
            for shape in (velocity.shape, stress.shape, rigidity.shape, (nodes * ny, width))
        ]
        + [jax.ShapeDtypeStruct(x.shape, f32) for x in rest[1:]],
        scratch_shapes=[
            pltpu.SMEM(cone.shape, jnp.int32),
            pltpu.VMEM(history.shape, history.dtype),
            pltpu.VMEM(kernel.shape, kernel.dtype),
            pltpu.SemaphoreType.DMA((4,)),
            pltpu.SemaphoreType.DMA((2, surfaces)),
            pltpu.SemaphoreType.DMA((len(rest),)),
        ],
        compiler_params=pltpu.CompilerParams(vmem_limit_bytes=FIRST_LIMIT),
    )(*(pinned(x) for x in (velocity, stress, rigidity, cone, history, kernel, *rest)))


def packed_into(target, parts):
    base, powers = 0, []
    for part in parts:
        size = part.shape[0]
        most = jnp.max(jnp.abs(part), axis=0, keepdims=True)
        power = jnp.ceil(jnp.log2(jnp.maximum(most, 2.0**-100)))
        powers.append(power)
        target[base : base + size] = jnp.round(part * jnp.exp2(14.0 - power)).astype(jnp.int16)
        base += size
    powers.append(jnp.zeros((16 - len(powers), powers[0].shape[1]), jnp.float32))
    target[base : base + 16] = jnp.concatenate(powers, axis=0).astype(jnp.int16)
    if target.shape[0] > base + 16:
        target[base + 16 :] = jnp.zeros_like(target[base + 16 :])


def unpacked(source, nodes):
    sizes = (nodes, nodes, 16, 16, 16)
    base, parts = 0, []
    last = sum(sizes)
    scales = jnp.exp2(source[last : last + 16].astype(jnp.float32) - 14.0)
    for place, size in enumerate(sizes):
        part = source[base : base + size].astype(jnp.float32)
        parts.append(part * scales[place : place + 1])
        base += size
    return parts


def relay_kernel(near, received, own, *refs):
    target = refs[-1]
    even, chip_even, _ = parities()
    to_right = chip_even if near else jnp.logical_not(chip_even)
    nodes = own.shape[1] // 3
    parts = []
    for surface in range(2):
        base = surface * 2 * nodes
        from_left = received[base : base + nodes]
        from_right = received[base + nodes : base + 2 * nodes]
        nothing = jnp.zeros_like(from_left)
        left = own[surface, :nodes] + lax.select(even, nothing, from_left)
        right = own[surface, 2 * nodes :] + lax.select(even, from_right, nothing)
        parts.append(lax.select(to_right, right, left))
    base = 4 * nodes
    halo = lax.select(to_right, received[base + 48 :], received[base : base + 48])
    packed_into(target, parts + [halo[at : at + 16] for at in (0, 16, 32)])


def relay_call(near, received, own, *after):
    nodes, width = own.shape[1] // 3, own.shape[2]
    rows = 2 * nodes + 64 + (0 if near else SPARE)
    return pl.pallas_call(
        functools.partial(relay_kernel, near),
        out_shape=jax.ShapeDtypeStruct((rows, width), jnp.int16),
        compiler_params=pltpu.CompilerParams(vmem_limit_bytes=4 * MIB),
    )(received, own, *after)


def beside(ref, at):
    nodes = ref.shape[0]
    up = ref[at + 1 : min(at + CHUNK + 1, nodes)]
    down = ref[max(at - 1, 0) : at + CHUNK - 1]
    nothing = jnp.zeros((1, *ref.shape[1:]), jnp.float32)
    if at + CHUNK == nodes:
        up = jnp.concatenate([up, nothing], axis=0)
    if at == 0:
        down = jnp.concatenate([nothing, down], axis=0)
    return up, down


def inner_kernel(last, *refs):
    velocity, stress, stress_y, rigidity, buoyancy = refs[:5]
    if last:
        stiffness, moved, stress_new, faces_new = refs[5:]
    else:
        moved, stress_new, faces_new, stiffness = refs[5:]
    nodes, ny, width = velocity.shape
    scale = courant * 0.5
    shape = (CHUNK, ny, width)
    lane = lane_of(shape)
    level = lax.broadcasted_iota(jnp.int32, shape, 1)

    def across(value):
        after = jnp.where(lane == width - 1, 0.0, turned(value, -1))
        before = jnp.where(lane == 0, 0.0, turned(value, 1))
        return after - before

    def stresses(at):
        cells = slice(at, at + CHUNK)
        here, rigid = velocity[cells], rigidity[cells]
        up, down = beside(velocity, at)
        stress_new[0, cells] = stress[0, cells] + scale * rigid * (up - down)
        stress_z = stress[1, cells] + scale * rigid * across(here)
        stress_new[1, cells] = stress_z
        if last:
            faces, stiff = stress_y[cells], stiffness[cells]
        else:
            faces = jnp.stack(
                [stress_y[pl.ds(at + r, ny, stride=nodes), :] for r in range(CHUNK)]
            )
            stiff = courant * (0.5 * (pltpu.roll(rigid, ny - 1, 1) + rigid))
            stiffness[cells] = stiff
        trial = faces + stiff * (pltpu.roll(here, ny - 1, 1) - here)
        trial = jnp.where(level == ny - 1, 0.0, trial)
        if last:
            for r in range(CHUNK):
                faces_new[pl.ds(at + r, ny, stride=nodes), :] = trial[r]
        else:
            faces_new[cells] = trial
        return 0.5 * across(stress_z) + trial - pltpu.roll(trial, 1, 1)

    def velocities(at, partial):
        cells = slice(at, at + CHUNK)
        up, down = beside(stress_new.at[0], at)
        moved[cells] = velocity[cells] + courant * buoyancy[cells] * (0.5 * (up - down) + partial)

    partial = stresses(0)
    for at in range(CHUNK, nodes, CHUNK):
        following = stresses(at)
        velocities(at - CHUNK, partial)
        partial = following
    velocities(nodes - CHUNK, partial)


def inner_call(last, *args):
    nodes, ny, width = args[0].shape
    shapes = [(nodes, ny, width), (2, nodes, ny, width)]
    shapes += [(nodes * ny, width)] if last else [(nodes, ny, width)] * 2
    return pl.pallas_call(
        functools.partial(inner_kernel, last),
        out_shape=[jax.ShapeDtypeStruct(shape, jnp.float32) for shape in shapes],
        out_specs=[pl.BlockSpec(memory_space=pltpu.VMEM)] * len(shapes),
        compiler_params=pltpu.CompilerParams(vmem_limit_bytes=8 * MIB),
    )(*args)


def step_kernel(last, *refs):
    (moved, stress, faces, velocity, rigidity, buoyancy) = refs[:6]
    (sigma_star, sigma_zero, friction) = refs[6:9]
    (received, near, far, depth_own, depth_near, depth_far, own) = refs[9:16]
    refs = refs[16:]
    nodes, ny, width = velocity.shape
    chunks = nodes // CHUNK
    fault = ny // 2 - 1
    scale = courant * 0.5
    copies = []
    if last:
        results, (velocity_new, shear, tips, broken, state_new, bounds), sems = (
            refs[:5],
            refs[5:11],
            refs[11],
        )

        def send(source, target):
            copies.append(pltpu.make_async_copy(source, target, sems.at[len(copies)]))
            copies[-1].start()

        inner = pl.ds(1, nodes - 2)
        send(stress.at[0, inner], results[1].at[0, inner])
        base = fault * nodes
        send(faces.at[pl.ds(0, base)], results[2].at[pl.ds(0, base)])
        above = pl.ds(base + nodes, (ny - 2 - fault) * nodes)
        send(faces.at[above], results[2].at[above])
    else:
        later, lead = refs[:2]
        velocity_new, stress_new, faces_new, state_new, core, own_new, edges = refs[2:9]
        edges_sent = refs[9]
        shear = stress_new.at[1]
    even, chip_even, _ = parities()

    def level_of(ref, y):
        return ref.reshape(nodes * ny, width)[pl.ds(y, nodes, stride=ny), :]

    near_parts, far_parts = unpacked(near, nodes), unpacked(far, nodes)
    traction = []
    for surface in range(2):
        base = surface * 2 * nodes
        mate = lax.select(
            even, received[base : base + nodes], received[base + nodes : base + 2 * nodes]
        )
        traction.append(
            own[surface, nodes : 2 * nodes] + mate + (near_parts[surface] + far_parts[surface])
        )

    near_halo, far_halo = (jnp.concatenate(x[2:], axis=0) for x in (near_parts, far_parts))
    left = lax.select(
        even, lax.select(chip_even, far_halo, near_halo), received[4 * nodes + 48 :]
    )
    right = lax.select(
        even, received[4 * nodes : 4 * nodes + 48], lax.select(chip_even, near_halo, far_halo)
    )
    stress_left = left[32:] + scale * left[16:32] * velocity[0]
    stress_right = right[32:] - scale * right[16:32] * velocity[nodes - 1]
    added_left = -scale * rigidity[0] * left[:16]
    added_right = scale * rigidity[nodes - 1] * right[:16]

    shape = (CHUNK, ny, width)
    sides = depth_sides(depth_own[...], depth_near[...], depth_far[...], chunks).reshape(shape)
    lane = lane_of(shape)
    edge = (lane == 0) | (lane == width - 1)
    margin = (lane < 2) | (lane >= width - 2)

    for at in range(0, nodes, CHUNK):
        cells = slice(at, at + CHUNK)
        place = 8 * (at // CHUNK)
        extra = jnp.where(margin, turned(sides, -(place + 2)), 0.0)
        velocity_new[cells] = moved[cells] + courant * buoyancy[cells] * extra
        extra = jnp.where(edge, turned(sides, -(place + 5)), 0.0)
        shear[cells] = stress[1, cells] + extra
        if last and (at + CHUNK) % (nodes // 2) == 0:
            half = pl.ds(at + CHUNK - nodes // 2, nodes // 2)
            send(shear.at[half], results[1].at[1, half])
        if not last:
            stress_new[0, cells] = stress[0, cells]
            faces_new[cells] = faces[cells]

    first_row, last_row = stress[0, 0] + added_left, stress[0, nodes - 1] + added_right
    if last:
        tips[0], tips[1] = first_row, last_row
        send(tips.at[0], results[1].at[0, 0])
        send(tips.at[1], results[1].at[0, nodes - 1])
    else:
        stress_new[0, 0], stress_new[0, nodes - 1] = first_row, last_row

    row = lax.broadcasted_iota(jnp.int32, (nodes, width), 0)
    lower, upper = slice(fault, fault + 1), slice(fault + 1, fault + 2)
    across = level_of(stress.at[0], fault + 1) - level_of(stress.at[0], fault)
    across = across + jnp.where(row == 0, added_left[upper] - added_left[lower], 0.0)
    across = across + jnp.where(row == nodes - 1, added_right[upper] - added_right[lower], 0.0)
    slip_rate = level_of(velocity, fault + 1) - level_of(velocity, fault)
    normal = sigma_zero[...] + bimaterial * jnp.tanh(across)
    state = normal + (sigma_star[...] - normal) * jnp.exp(
        -(jnp.abs(slip_rate) + slip_ref) * decay_rate
    )
    state_new[...] = state
    strength = friction[...] * state
    trial = faces[fault * nodes : (fault + 1) * nodes] if last else level_of(faces, fault)
    clipped = jnp.clip(trial, -strength, strength)
    bottom = traction[0] + impedance * level_of(velocity, 0)
    top = traction[1] - impedance * level_of(velocity, ny - 1)
    if last:
        broken[...] = clipped
        bounds[0], bounds[1] = bottom, top
        send(broken, results[2].at[pl.ds(fault * nodes, nodes)])
        send(state_new, results[3])
        send(bounds, results[4])
    else:
        faces_new.reshape(nodes * ny, width)[pl.ds(fault, nodes, stride=ny), :] = clipped

    flat = velocity_new.reshape(nodes * ny, width)
    for y, change in (
        (fault, clipped - trial),
        (fault + 1, trial - clipped),
        (0, -bottom),
        (ny - 1, top),
    ):
        at = pl.ds(y, nodes, stride=ny)
        flat[at, :] = flat[at, :] + courant * level_of(buoyancy, y) * change
    for x, change in (
        (0, -stress_left),
        (1, -added_left),
        (nodes - 2, added_right),
        (nodes - 1, stress_right),
    ):
        velocity_new[x] = velocity_new[x] + (0.5 * courant) * buoyancy[x] * change

    if last:
        send(velocity_new, results[0])
        for copy in copies:
            copy.wait()
        return

    for surface in range(2):
        fresh = level_of(velocity_new, surface * (ny - 1)).astype(jnp.bfloat16)
        total = later[surface] + jnp.dot(
            lead[surface], fresh, preferred_element_type=jnp.float32
        )
        deal(total, core, own_new, surface)
    strike_edge(
        core, 4 * nodes, velocity_new[0], rigidity[0], stress_new[0, 0], velocity_new[1], 1.0
    )
    strike_edge(
        core,
        4 * nodes + 48,
        velocity_new[nodes - 1],
        rigidity[nodes - 1],
        stress_new[0, nodes - 1],
        velocity_new[nodes - 2],
        -1.0,
    )
    cells = [slice(at, at + CHUNK) for at in range(0, nodes, CHUNK)]
    depth_edges(edges, edges_sent, [(velocity_new[c], stress_new[1, c], rigidity[c]) for c in cells])


def step_call(last, *args):
    nodes, ny, width = args[0].shape
    f32 = jnp.float32
    shapes = [(nodes, ny, width), (2, nodes, ny, width)]
    if last:
        shapes += [(nodes * (ny - 1), width), (nodes, width), (2, nodes, width)]
        held = [(nodes, ny, width)] * 2 + [(2, ny, width), (nodes, width), *shapes[3:]]
        scratch = [pltpu.VMEM(shape, f32) for shape in held]
        scratch += [pltpu.SemaphoreType.DMA((11,))]
        space = pltpu.HBM
    else:
        shapes += [
            (nodes, ny, width),
            (nodes, width),
            (4 * nodes + 96, width),
            (2, 3 * nodes, width),
            (8, nodes * ny),
        ]
        scratch, space = [], pltpu.VMEM
    out_shape = [jax.ShapeDtypeStruct(shape, f32) for shape in shapes]
    if not last:
        out_shape.append(jax.ShapeDtypeStruct((nodes, width), jnp.bfloat16))
    return pl.pallas_call(
        functools.partial(step_kernel, last),
        out_shape=out_shape,
        out_specs=[pl.BlockSpec(memory_space=space)] * len(out_shape),
        scratch_shapes=scratch,
        compiler_params=pltpu.CompilerParams(vmem_limit_bytes=16 * MIB),
    )(*args)


def exchange(core, own, edges, edges_sent):
    received = lax.ppermute(core, GX, swap_pairs(GX, 1, 0))
    depth_near = lax.ppermute(edges_sent, GZ, swap_pairs(GZ, 1, 0))
    far = lax.ppermute(relay_call(False, received, own), GX, swap_pairs(GX, 2, 2))
    near = relay_call(True, received, own, depth_near)
    near = lax.ppermute(near, GX, swap_pairs(GX, 2, 0))
    depth_far = lax.ppermute(depth_near, GZ, onward_pairs(GZ))
    return received, near, far, edges, depth_near, depth_far


def local(
    velocity,
    stress_xz,
    stress_y,
    rigidity,
    buoyancy,
    sigma_star,
    sigma_zero,
    friction,
    history,
    kernel,
    cone,
):
    surfaces, lags, nodes, width = history.shape
    faces = stress_y.shape[1]
    past = history.reshape(surfaces, lags * nodes, width)
    matrix = kernel.reshape(surfaces, -1, kernel.shape[3])
    turned_cone = jnp.transpose(cone, (0, 2, 3, 1))
    face_rows = jnp.transpose(stress_y, (1, 0, 2)).reshape(faces * nodes, width)
    core, own, later, lead, edges, sent, velocity, stress_xz, rigidity, *rest = first_call(
        velocity,
        stress_xz,
        rigidity,
        turned_cone,
        past,
        matrix,
        face_rows,
        buoyancy,
        sigma_star,
        sigma_zero,
        friction,
    )
    face_rows, buoyancy, sigma_star, sigma_zero, friction = rest
    *inner, stiffness = inner_call(False, velocity, stress_xz, face_rows, rigidity, buoyancy)
    velocity, stress_xz, stress_y, state, core, own, edges, sent = step_call(
        False,
        *inner,
        velocity,
        rigidity,
        buoyancy,
        sigma_star,
        sigma_zero,
        friction,
        *exchange(core, own, edges, sent),
        own,
        later,
        lead,
    )
    inner = inner_call(True, velocity, stress_xz, stress_y, rigidity, buoyancy, stiffness)
    velocity, stress_xz, face_rows, state, bounds = step_call(
        True,
        *inner,
        velocity,
        rigidity,
        buoyancy,
        state,
        sigma_zero,
        friction,
        *exchange(core, own, edges, sent),
        own,
    )
    stress_y = jnp.transpose(face_rows.reshape(faces, nodes, width), (1, 0, 2))
    return velocity, stress_xz, stress_y, state, bounds


def solution(mesh):
    in_specs = (
        P("gx", None, "gz"),
        P(None, "gx", None, "gz"),
        P("gx", None, "gz"),
        P("gx", None, "gz"),
        P("gx", None, "gz"),
        P("gx", "gz"),
        P("gx", "gz"),
        P("gx", "gz"),
        P(None, None, "gx", "gz"),
        P(),
        P(),
    )
    out_specs = (
        P("gx", None, "gz"),
        P(None, "gx", None, "gz"),
        P("gx", None, "gz"),
        P("gx", "gz"),
        P(None, "gx", "gz"),
    )
    return jax.shard_map(
        local, mesh=mesh, in_specs=in_specs, out_specs=tuple(out_specs), check_vma=False
    )
```

```python
import functools

import jax
import jax.numpy as jnp
from jax import lax
from jax.experimental import pallas as pl
from jax.experimental.pallas import tpu as pltpu
from jax.sharding import PartitionSpec as P

courant = 0.25
bimaterial = 0.5
slip_ref = 0.2
decay_rate = 0.5
impedance = 0.5

GX, GZ = "gx", "gz"
CHUNK = 8
CHUNK_COLUMNS = 1024
SPLIT = 2
SPARE = 32
MIB = 2**20
FIRST_LIMIT = 12 * MIB


def swap_pairs(axis, distance, phase):
    size, pairs = lax.axis_size(axis), []
    for i in range(size):
        partner = i + distance if (i - phase) % (2 * distance) < distance else i - distance
        if 0 <= partner < size:
            pairs.append((i, partner))
    return pairs


def onward_pairs(axis):
    size, pairs = lax.axis_size(axis), []
    for i in range(size):
        partner = i + 2 if i % 2 == 0 else i - 2
        if 0 <= partner < size:
            pairs.append((i, partner))
    return pairs


def parities():
    block = lax.axis_index(GX)
    even = lax.rem(block, 2) == 0
    chip_even = lax.rem(lax.div(block, 2), 2) == 0
    depth_even = lax.rem(lax.axis_index(GZ), 2) == 0
    return even, chip_even, depth_even


def lane_of(shape):
    return lax.broadcasted_iota(jnp.int32, shape, len(shape) - 1)


def turned(value, shift):
    return pltpu.roll(value, shift % value.shape[-1], value.ndim - 1)


def depth_edges(edges, edges_sent, cells):
    packed, group = None, 8
    for place, (velocity, stress_z, rigidity) in enumerate(cells):
        base = place * group
        lane = lane_of(velocity.shape)
        if packed is None:
            packed = jnp.zeros(velocity.shape, velocity.dtype)
        packed = jnp.where(
            lane < base,
            packed,
            jnp.where(
                lane < base + 4,
                turned(velocity, base + 2),
                jnp.where(lane < base + 6, turned(stress_z, base + 5), turned(rigidity, base + 7)),
            ),
        )
    size = packed.shape[0] * packed.shape[1]
    rows = packed.reshape(size, -1).T
    for place in range(len(cells)):
        edges[:, place * size : (place + 1) * size] = rows[place * group : (place + 1) * group]
    edges_sent[...] = rows[: edges_sent.shape[0]].astype(edges_sent.dtype)


def depth_sides(own, near, far, chunks):
    _, _, depth_even = parities()
    near, far = (
        jnp.concatenate([x[at : at + 8] for at in range(0, x.shape[0], 8)], axis=1)
        for x in (near.astype(jnp.float32), far.astype(jnp.float32))
    )
    left = lax.select(depth_even, far, near)
    right = lax.select(depth_even, near, far)
    scale = courant * 0.5
    stress_left = left[4:5] + scale * left[6:7] * (own[2:3] - left[0:1])
    stress_right = right[5:6] + scale * right[7:8] * (right[3:4] - own[1:2])
    first = -scale * own[7:8] * left[1:2]
    last = scale * own[6:7] * right[2:3]
    nothing = jnp.zeros_like(first)
    rows = [0.5 * last, 0.5 * stress_right, -0.5 * stress_left, -0.5 * first]
    rows = jnp.concatenate([*rows, last, first, nothing, nothing], axis=0)
    size = rows.shape[1] // chunks
    pieces = [rows[:, place * size : (place + 1) * size] for place in range(chunks)]
    pieces.append(jnp.zeros((size - 8 * chunks, size), rows.dtype))
    return jnp.concatenate(pieces, axis=0).T


def strike_edge(target, base, velocity, rigidity, stress_x, inner, sign):
    target[base : base + 16] = velocity
    target[base + 16 : base + 32] = rigidity
    target[base + 32 : base + 48] = stress_x + (sign * courant * 0.5) * rigidity * inner


def deal(total, core, own, surface):
    nodes = total.shape[0] // 5
    for place, index in enumerate((0, 2, 4)):
        own[surface, place * nodes : (place + 1) * nodes] = total[
            index * nodes : (index + 1) * nodes
        ]
    base = surface * 2 * nodes
    core[base : base + nodes] = total[nodes : 2 * nodes]
    core[base + nodes : base + 2 * nodes] = total[3 * nodes : 4 * nodes]


def first_kernel(*refs):
    (velocity, stress, rigidity, cone, history, kernel), rest = refs[:6], refs[6:11]
    core, own, later, lead, edges, edges_sent, speed, tension, rigid = refs[11:20]
    rest_held = refs[20:25]
    limits, past, matrix, slab_sems, part_sems, rest_sems = refs[25:]
    surfaces, rows, columns = kernel.shape
    nodes, ny, width = velocity.shape
    offsets = rows // nodes
    reach = (offsets - 1) // 2
    parts = columns // CHUNK_COLUMNS

    slab = [
        pltpu.make_async_copy(source, target, slab_sems.at[place])
        for place, (source, target) in enumerate(
            ((cone, limits), (velocity, speed), (rigidity, rigid), (stress, tension))
        )
    ]
    piece = columns // SPLIT
    fetches = []
    for surface in range(surfaces):
        for half in range(SPLIT):
            place, span = len(fetches), pl.ds(half * piece, piece)
            fetches.append(
                (
                    pltpu.make_async_copy(
                        history.at[surface, span], past.at[surface, span], part_sems.at[0, place]
                    ),
                    pltpu.make_async_copy(
                        kernel.at[surface, :, span],
                        matrix.at[surface, :, span],
                        part_sems.at[1, place],
                    ),
                )
            )
    others = [
        pltpu.make_async_copy(source, target.at[pl.ds(0, source.shape[0])], rest_sems.at[place])
        for place, (source, target) in enumerate(zip(rest, rest_held))
    ]
    following = {0: (*fetches[3], *slab[1:]), 1: others}
    for copy in (slab[0], *fetches[0], *fetches[1]):
        copy.start()
    slab[0].wait()
    for copy in fetches[2]:
        copy.start()

    block = lax.axis_index(GX)
    blocks = cone.shape[3]
    lag = lax.div(lane_of((1, CHUNK_COLUMNS)), nodes)
    order = [(surface, part) for surface in range(surfaces) for part in range(parts)]
    for surface, part in order:
        at = part * CHUNK_COLUMNS
        if at % piece == 0:
            place = surface * SPLIT + at // piece
            for copy in fetches[place]:
                copy.wait()
            for copy in following.get(place, ()):
                copy.start()
        if (surface, part) == order[-1]:
            for copy in slab[1:]:
                copy.wait()
            cells = [slice(at, at + CHUNK) for at in range(0, nodes, CHUNK)]
            depth_edges(edges, edges_sent, [(speed[c], tension[1, c], rigid[c]) for c in cells])
            base = 4 * nodes
            strike_edge(core, base, speed[0], rigid[0], tension[0, 0], speed[1], 1.0)
            strike_edge(
                core,
                base + 48,
                speed[nodes - 1],
                rigid[nodes - 1],
                tension[0, nodes - 1],
                speed[nodes - 2],
                -1.0,
            )
        masked = []
        for index in range(offsets):
            target = jnp.clip(block + (index - reach), 0, blocks - 1)
            first = limits[surface, index, 0, target]
            last = limits[surface, index, 1, target]
            now = lag + at // nodes
            keep = jnp.where((now >= first) & (now < last), 1.0, 0.0).astype(jnp.bfloat16)
            masked.append(
                matrix[surface, index * nodes : (index + 1) * nodes, at : at + CHUNK_COLUMNS]
                * keep
            )
        kept = jnp.concatenate(masked, axis=0)
        now = past[surface, at : at + CHUNK_COLUMNS]
        if part:
            before = past[surface, at - nodes : at + CHUNK_COLUMNS - nodes]
        else:
            before = jnp.concatenate(
                [jnp.zeros((nodes, width), now.dtype), now[: CHUNK_COLUMNS - nodes]], axis=0
            )
            lead[surface] = kept[:, :nodes]
        both = jnp.concatenate([now, before], axis=1)
        product = jnp.dot(kept, both, preferred_element_type=jnp.float32)
        total = total + product if part else product
        if part == parts - 1:
            later[surface] = total[:, width:]
            deal(total[:, :width], core, own, surface)
    for copy in others:
        copy.wait()


def pinned(x):
    return pltpu.with_memory_space_constraint(x, pltpu.HBM)


def first_call(velocity, stress, rigidity, cone, history, kernel, *rest):
    surfaces, rows, columns = kernel.shape
    nodes, ny, width = velocity.shape
    f32 = jnp.float32
    return pl.pallas_call(
        first_kernel,
        in_specs=[pl.BlockSpec(memory_space=pltpu.HBM)] * (6 + len(rest)),
        out_specs=[pl.BlockSpec(memory_space=pltpu.VMEM)] * (9 + len(rest)),
        out_shape=[
            jax.ShapeDtypeStruct((4 * nodes + 96, width), f32),
            jax.ShapeDtypeStruct((surfaces, 3 * nodes, width), f32),
            jax.ShapeDtypeStruct((surfaces, rows, width), f32),
            jax.ShapeDtypeStruct((surfaces, rows, nodes), jnp.bfloat16),
            jax.ShapeDtypeStruct((8, nodes * ny), f32),
            jax.ShapeDtypeStruct((nodes, width), jnp.bfloat16),
        ]
        + [
            jax.ShapeDtypeStruct(shape, f32)
            for shape in (velocity.shape, stress.shape, rigidity.shape, (nodes * ny, width))
        ]
        + [jax.ShapeDtypeStruct(x.shape, f32) for x in rest[1:]],
        scratch_shapes=[
            pltpu.SMEM(cone.shape, jnp.int32),
            pltpu.VMEM(history.shape, history.dtype),
            pltpu.VMEM(kernel.shape, kernel.dtype),
            pltpu.SemaphoreType.DMA((4,)),
            pltpu.SemaphoreType.DMA((2, surfaces * SPLIT)),
            pltpu.SemaphoreType.DMA((len(rest),)),
        ],
        compiler_params=pltpu.CompilerParams(vmem_limit_bytes=FIRST_LIMIT),
    )(*(pinned(x) for x in (velocity, stress, rigidity, cone, history, kernel, *rest)))


def packed_into(target, parts):
    base, powers = 0, []
    for part in parts:
        size = part.shape[0]
        most = jnp.max(jnp.abs(part), axis=0, keepdims=True)
        power = jnp.ceil(jnp.log2(jnp.maximum(most, 2.0**-100)))
        powers.append(power)
        target[base : base + size] = jnp.round(part * jnp.exp2(14.0 - power)).astype(jnp.int16)
        base += size
    powers.append(jnp.zeros((16 - len(powers), powers[0].shape[1]), jnp.float32))
    target[base : base + 16] = jnp.concatenate(powers, axis=0).astype(jnp.int16)
    if target.shape[0] > base + 16:
        target[base + 16 :] = jnp.zeros_like(target[base + 16 :])


def unpacked(source, nodes):
    sizes = (nodes, nodes, 16, 16, 16)
    base, parts = 0, []
    last = sum(sizes)
    scales = jnp.exp2(source[last : last + 16].astype(jnp.float32) - 14.0)
    for place, size in enumerate(sizes):
        part = source[base : base + size].astype(jnp.float32)
        parts.append(part * scales[place : place + 1])
        base += size
    return parts


def relay_kernel(near, received, own, *refs):
    target = refs[-1]
    even, chip_even, _ = parities()
    to_right = chip_even if near else jnp.logical_not(chip_even)
    nodes = own.shape[1] // 3
    parts = []
    for surface in range(2):
        base = surface * 2 * nodes
        from_left = received[base : base + nodes]
        from_right = received[base + nodes : base + 2 * nodes]
        nothing = jnp.zeros_like(from_left)
        left = own[surface, :nodes] + lax.select(even, nothing, from_left)
        right = own[surface, 2 * nodes :] + lax.select(even, from_right, nothing)
        parts.append(lax.select(to_right, right, left))
    base = 4 * nodes
    halo = lax.select(to_right, received[base + 48 :], received[base : base + 48])
    packed_into(target, parts + [halo[at : at + 16] for at in (0, 16, 32)])


def relay_call(near, received, own, *after):
    nodes, width = own.shape[1] // 3, own.shape[2]
    rows = 2 * nodes + 64 + (0 if near else SPARE)
    return pl.pallas_call(
        functools.partial(relay_kernel, near),
        out_shape=jax.ShapeDtypeStruct((rows, width), jnp.int16),
        compiler_params=pltpu.CompilerParams(vmem_limit_bytes=4 * MIB),
    )(received, own, *after)


def beside(ref, at):
    nodes = ref.shape[0]
    up = ref[at + 1 : min(at + CHUNK + 1, nodes)]
    down = ref[max(at - 1, 0) : at + CHUNK - 1]
    nothing = jnp.zeros((1, *ref.shape[1:]), jnp.float32)
    if at + CHUNK == nodes:
        up = jnp.concatenate([up, nothing], axis=0)
    if at == 0:
        down = jnp.concatenate([nothing, down], axis=0)
    return up, down


def inner_kernel(last, *refs):
    velocity, stress, stress_y, rigidity, buoyancy = refs[:5]
    if last:
        stiffness, moved, stress_new, faces_new = refs[5:]
    else:
        moved, stress_new, faces_new, stiffness = refs[5:]
    nodes, ny, width = velocity.shape
    scale = courant * 0.5
    shape = (CHUNK, ny, width)
    lane = lane_of(shape)
    level = lax.broadcasted_iota(jnp.int32, shape, 1)

    def across(value):
        after = jnp.where(lane == width - 1, 0.0, turned(value, -1))
        before = jnp.where(lane == 0, 0.0, turned(value, 1))
        return after - before

    def stresses(at):
        cells = slice(at, at + CHUNK)
        here, rigid = velocity[cells], rigidity[cells]
        up, down = beside(velocity, at)
        stress_new[0, cells] = stress[0, cells] + scale * rigid * (up - down)
        stress_z = stress[1, cells] + scale * rigid * across(here)
        stress_new[1, cells] = stress_z
        if last:
            faces, stiff = stress_y[cells], stiffness[cells]
        else:
            faces = jnp.stack(
                [stress_y[pl.ds(at + r, ny, stride=nodes), :] for r in range(CHUNK)]
            )
            stiff = courant * (0.5 * (pltpu.roll(rigid, ny - 1, 1) + rigid))
            stiffness[cells] = stiff
        trial = faces + stiff * (pltpu.roll(here, ny - 1, 1) - here)
        trial = jnp.where(level == ny - 1, 0.0, trial)
        if last:
            for r in range(CHUNK):
                faces_new[pl.ds(at + r, ny, stride=nodes), :] = trial[r]
        else:
            faces_new[cells] = trial
        return 0.5 * across(stress_z) + trial - pltpu.roll(trial, 1, 1)

    def velocities(at, partial):
        cells = slice(at, at + CHUNK)
        up, down = beside(stress_new.at[0], at)
        moved[cells] = velocity[cells] + courant * buoyancy[cells] * (0.5 * (up - down) + partial)

    partial = stresses(0)
    for at in range(CHUNK, nodes, CHUNK):
        following = stresses(at)
        velocities(at - CHUNK, partial)
        partial = following
    velocities(nodes - CHUNK, partial)


def inner_call(last, *args):
    nodes, ny, width = args[0].shape
    shapes = [(nodes, ny, width), (2, nodes, ny, width)]
    shapes += [(nodes * ny, width)] if last else [(nodes, ny, width)] * 2
    return pl.pallas_call(
        functools.partial(inner_kernel, last),
        out_shape=[jax.ShapeDtypeStruct(shape, jnp.float32) for shape in shapes],
        out_specs=[pl.BlockSpec(memory_space=pltpu.VMEM)] * len(shapes),
        compiler_params=pltpu.CompilerParams(vmem_limit_bytes=8 * MIB),
    )(*args)


def step_kernel(last, *refs):
    (moved, stress, faces, velocity, rigidity, buoyancy) = refs[:6]
    (sigma_star, sigma_zero, friction) = refs[6:9]
    (received, near, far, depth_own, depth_near, depth_far, own) = refs[9:16]
    refs = refs[16:]
    nodes, ny, width = velocity.shape
    chunks = nodes // CHUNK
    fault = ny // 2 - 1
    scale = courant * 0.5
    copies = []
    if last:
        results, (velocity_new, shear, tips, broken, state_new, bounds), sems = (
            refs[:5],
            refs[5:11],
            refs[11],
        )

        def send(source, target):
            copies.append(pltpu.make_async_copy(source, target, sems.at[len(copies)]))
            copies[-1].start()

        inner = pl.ds(1, nodes - 2)
        send(stress.at[0, inner], results[1].at[0, inner])
        base = fault * nodes
        send(faces.at[pl.ds(0, base)], results[2].at[pl.ds(0, base)])
        above = pl.ds(base + nodes, (ny - 2 - fault) * nodes)
        send(faces.at[above], results[2].at[above])
    else:
        later, lead = refs[:2]
        velocity_new, stress_new, faces_new, state_new, core, own_new, edges = refs[2:9]
        edges_sent = refs[9]
        shear = stress_new.at[1]
    even, chip_even, _ = parities()

    def level_of(ref, y):
        return ref.reshape(nodes * ny, width)[pl.ds(y, nodes, stride=ny), :]

    near_parts, far_parts = unpacked(near, nodes), unpacked(far, nodes)
    traction = []
    for surface in range(2):
        base = surface * 2 * nodes
        mate = lax.select(
            even, received[base : base + nodes], received[base + nodes : base + 2 * nodes]
        )
        traction.append(
            own[surface, nodes : 2 * nodes] + mate + (near_parts[surface] + far_parts[surface])
        )

    near_halo, far_halo = (jnp.concatenate(x[2:], axis=0) for x in (near_parts, far_parts))
    left = lax.select(
        even, lax.select(chip_even, far_halo, near_halo), received[4 * nodes + 48 :]
    )
    right = lax.select(
        even, received[4 * nodes : 4 * nodes + 48], lax.select(chip_even, near_halo, far_halo)
    )
    stress_left = left[32:] + scale * left[16:32] * velocity[0]
    stress_right = right[32:] - scale * right[16:32] * velocity[nodes - 1]
    added_left = -scale * rigidity[0] * left[:16]
    added_right = scale * rigidity[nodes - 1] * right[:16]

    shape = (CHUNK, ny, width)
    sides = depth_sides(depth_own[...], depth_near[...], depth_far[...], chunks).reshape(shape)
    lane = lane_of(shape)
    edge = (lane == 0) | (lane == width - 1)
    margin = (lane < 2) | (lane >= width - 2)

    for at in range(0, nodes, CHUNK):
        cells = slice(at, at + CHUNK)
        place = 8 * (at // CHUNK)
        extra = jnp.where(margin, turned(sides, -(place + 2)), 0.0)
        velocity_new[cells] = moved[cells] + courant * buoyancy[cells] * extra
        extra = jnp.where(edge, turned(sides, -(place + 5)), 0.0)
        shear[cells] = stress[1, cells] + extra
        if last and (at + CHUNK) % (nodes // 2) == 0:
            half = pl.ds(at + CHUNK - nodes // 2, nodes // 2)
            send(shear.at[half], results[1].at[1, half])
        if not last:
            stress_new[0, cells] = stress[0, cells]
            faces_new[cells] = faces[cells]

    first_row, last_row = stress[0, 0] + added_left, stress[0, nodes - 1] + added_right
    if last:
        tips[0], tips[1] = first_row, last_row
        send(tips.at[0], results[1].at[0, 0])
        send(tips.at[1], results[1].at[0, nodes - 1])
    else:
        stress_new[0, 0], stress_new[0, nodes - 1] = first_row, last_row

    row = lax.broadcasted_iota(jnp.int32, (nodes, width), 0)
    lower, upper = slice(fault, fault + 1), slice(fault + 1, fault + 2)
    across = level_of(stress.at[0], fault + 1) - level_of(stress.at[0], fault)
    across = across + jnp.where(row == 0, added_left[upper] - added_left[lower], 0.0)
    across = across + jnp.where(row == nodes - 1, added_right[upper] - added_right[lower], 0.0)
    slip_rate = level_of(velocity, fault + 1) - level_of(velocity, fault)
    normal = sigma_zero[...] + bimaterial * jnp.tanh(across)
    state = normal + (sigma_star[...] - normal) * jnp.exp(
        -(jnp.abs(slip_rate) + slip_ref) * decay_rate
    )
    state_new[...] = state
    strength = friction[...] * state
    trial = faces[fault * nodes : (fault + 1) * nodes] if last else level_of(faces, fault)
    clipped = jnp.clip(trial, -strength, strength)
    bottom = traction[0] + impedance * level_of(velocity, 0)
    top = traction[1] - impedance * level_of(velocity, ny - 1)
    if last:
        broken[...] = clipped
        bounds[0], bounds[1] = bottom, top
        send(broken, results[2].at[pl.ds(fault * nodes, nodes)])
        send(state_new, results[3])
        send(bounds, results[4])
    else:
        faces_new.reshape(nodes * ny, width)[pl.ds(fault, nodes, stride=ny), :] = clipped

    flat = velocity_new.reshape(nodes * ny, width)
    for y, change in (
        (fault, clipped - trial),
        (fault + 1, trial - clipped),
        (0, -bottom),
        (ny - 1, top),
    ):
        at = pl.ds(y, nodes, stride=ny)
        flat[at, :] = flat[at, :] + courant * level_of(buoyancy, y) * change
    for x, change in (
        (0, -stress_left),
        (1, -added_left),
        (nodes - 2, added_right),
        (nodes - 1, stress_right),
    ):
        velocity_new[x] = velocity_new[x] + (0.5 * courant) * buoyancy[x] * change

    if last:
        send(velocity_new, results[0])
        for copy in copies:
            copy.wait()
        return

    for surface in range(2):
        fresh = level_of(velocity_new, surface * (ny - 1)).astype(jnp.bfloat16)
        total = later[surface] + jnp.dot(
            lead[surface], fresh, preferred_element_type=jnp.float32
        )
        deal(total, core, own_new, surface)
    strike_edge(
        core, 4 * nodes, velocity_new[0], rigidity[0], stress_new[0, 0], velocity_new[1], 1.0
    )
    strike_edge(
        core,
        4 * nodes + 48,
        velocity_new[nodes - 1],
        rigidity[nodes - 1],
        stress_new[0, nodes - 1],
        velocity_new[nodes - 2],
        -1.0,
    )
    cells = [slice(at, at + CHUNK) for at in range(0, nodes, CHUNK)]
    depth_edges(edges, edges_sent, [(velocity_new[c], stress_new[1, c], rigidity[c]) for c in cells])


def step_call(last, *args):
    nodes, ny, width = args[0].shape
    f32 = jnp.float32
    shapes = [(nodes, ny, width), (2, nodes, ny, width)]
    if last:
        shapes += [(nodes * (ny - 1), width), (nodes, width), (2, nodes, width)]
        held = [(nodes, ny, width)] * 2 + [(2, ny, width), (nodes, width), *shapes[3:]]
        scratch = [pltpu.VMEM(shape, f32) for shape in held]
        scratch += [pltpu.SemaphoreType.DMA((11,))]
        space = pltpu.HBM
    else:
        shapes += [
            (nodes, ny, width),
            (nodes, width),
            (4 * nodes + 96, width),
            (2, 3 * nodes, width),
            (8, nodes * ny),
        ]
        scratch, space = [], pltpu.VMEM
    out_shape = [jax.ShapeDtypeStruct(shape, f32) for shape in shapes]
    if not last:
        out_shape.append(jax.ShapeDtypeStruct((nodes, width), jnp.bfloat16))
    return pl.pallas_call(
        functools.partial(step_kernel, last),
        out_shape=out_shape,
        out_specs=[pl.BlockSpec(memory_space=space)] * len(out_shape),
        scratch_shapes=scratch,
        compiler_params=pltpu.CompilerParams(vmem_limit_bytes=16 * MIB),
    )(*args)


def exchange(core, own, edges, edges_sent):
    received = lax.ppermute(core, GX, swap_pairs(GX, 1, 0))
    depth_near = lax.ppermute(edges_sent, GZ, swap_pairs(GZ, 1, 0))
    far = lax.ppermute(relay_call(False, received, own), GX, swap_pairs(GX, 2, 2))
    near = relay_call(True, received, own, depth_near)
    near = lax.ppermute(near, GX, swap_pairs(GX, 2, 0))
    depth_far = lax.ppermute(depth_near, GZ, onward_pairs(GZ))
    return received, near, far, edges, depth_near, depth_far


def local(
    velocity,
    stress_xz,
    stress_y,
    rigidity,
    buoyancy,
    sigma_star,
    sigma_zero,
    friction,
    history,
    kernel,
    cone,
):
    surfaces, lags, nodes, width = history.shape
    faces = stress_y.shape[1]
    past = history.reshape(surfaces, lags * nodes, width)
    matrix = kernel.reshape(surfaces, -1, kernel.shape[3])
    turned_cone = jnp.transpose(cone, (0, 2, 3, 1))
    face_rows = jnp.transpose(stress_y, (1, 0, 2)).reshape(faces * nodes, width)
    core, own, later, lead, edges, sent, velocity, stress_xz, rigidity, *rest = first_call(
        velocity,
        stress_xz,
        rigidity,
        turned_cone,
        past,
        matrix,
        face_rows,
        buoyancy,
        sigma_star,
        sigma_zero,
        friction,
    )
    face_rows, buoyancy, sigma_star, sigma_zero, friction = rest
    *inner, stiffness = inner_call(False, velocity, stress_xz, face_rows, rigidity, buoyancy)
    velocity, stress_xz, stress_y, state, core, own, edges, sent = step_call(
        False,
        *inner,
        velocity,
        rigidity,
        buoyancy,
        sigma_star,
        sigma_zero,
        friction,
        *exchange(core, own, edges, sent),
        own,
        later,
        lead,
    )
    inner = inner_call(True, velocity, stress_xz, stress_y, rigidity, buoyancy, stiffness)
    velocity, stress_xz, face_rows, state, bounds = step_call(
        True,
        *inner,
        velocity,
        rigidity,
        buoyancy,
        state,
        sigma_zero,
        friction,
        *exchange(core, own, edges, sent),
        own,
    )
    stress_y = jnp.transpose(face_rows.reshape(faces, nodes, width), (1, 0, 2))
    return velocity, stress_xz, stress_y, state, bounds


def solution(mesh):
    in_specs = (
        P("gx", None, "gz"),
        P(None, "gx", None, "gz"),
        P("gx", None, "gz"),
        P("gx", None, "gz"),
        P("gx", None, "gz"),
        P("gx", "gz"),
        P("gx", "gz"),
        P("gx", "gz"),
        P(None, None, "gx", "gz"),
        P(),
        P(),
    )
    out_specs = (
        P("gx", None, "gz"),
        P(None, "gx", None, "gz"),
        P("gx", None, "gz"),
        P("gx", "gz"),
        P(None, "gx", "gz"),
    )
    return jax.shard_map(
        local, mesh=mesh, in_specs=in_specs, out_specs=tuple(out_specs), check_vma=False
    )
```

```python
import functools

import jax
import jax.numpy as jnp
from jax import lax
from jax.experimental import pallas as pl
from jax.experimental.pallas import tpu as pltpu
from jax.sharding import PartitionSpec as P

courant = 0.25
bimaterial = 0.5
slip_ref = 0.2
decay_rate = 0.5
impedance = 0.5

GX, GZ = "gx", "gz"
CHUNK = 8
CHUNK_COLUMNS = 1024
SPLIT = 2
SPARE = 16
MIB = 2**20
FIRST_LIMIT = 12 * MIB


def swap_pairs(axis, distance, phase):
    size, pairs = lax.axis_size(axis), []
    for i in range(size):
        partner = i + distance if (i - phase) % (2 * distance) < distance else i - distance
        if 0 <= partner < size:
            pairs.append((i, partner))
    return pairs


def onward_pairs(axis):
    size, pairs = lax.axis_size(axis), []
    for i in range(size):
        partner = i + 2 if i % 2 == 0 else i - 2
        if 0 <= partner < size:
            pairs.append((i, partner))
    return pairs


def parities():
    block = lax.axis_index(GX)
    even = lax.rem(block, 2) == 0
    chip_even = lax.rem(lax.div(block, 2), 2) == 0
    depth_even = lax.rem(lax.axis_index(GZ), 2) == 0
    return even, chip_even, depth_even


def lane_of(shape):
    return lax.broadcasted_iota(jnp.int32, shape, len(shape) - 1)


def turned(value, shift):
    return pltpu.roll(value, shift % value.shape[-1], value.ndim - 1)


def depth_edges(edges, edges_sent, cells):
    packed, group = None, 8
    for place, (velocity, stress_z, rigidity) in enumerate(cells):
        base = place * group
        lane = lane_of(velocity.shape)
        if packed is None:
            packed = jnp.zeros(velocity.shape, velocity.dtype)
        packed = jnp.where(
            lane < base,
            packed,
            jnp.where(
                lane < base + 4,
                turned(velocity, base + 2),
                jnp.where(lane < base + 6, turned(stress_z, base + 5), turned(rigidity, base + 7)),
            ),
        )
    size = packed.shape[0] * packed.shape[1]
    rows = packed.reshape(size, -1).T
    for place in range(len(cells)):
        edges[:, place * size : (place + 1) * size] = rows[place * group : (place + 1) * group]
    edges_sent[...] = rows[: edges_sent.shape[0]].astype(edges_sent.dtype)


def depth_sides(own, near, far, chunks):
    _, _, depth_even = parities()
    near, far = (
        jnp.concatenate([x[at : at + 8] for at in range(0, x.shape[0], 8)], axis=1)
        for x in (near.astype(jnp.float32), far.astype(jnp.float32))
    )
    left = lax.select(depth_even, far, near)
    right = lax.select(depth_even, near, far)
    scale = courant * 0.5
    stress_left = left[4:5] + scale * left[6:7] * (own[2:3] - left[0:1])
    stress_right = right[5:6] + scale * right[7:8] * (right[3:4] - own[1:2])
    first = -scale * own[7:8] * left[1:2]
    last = scale * own[6:7] * right[2:3]
    nothing = jnp.zeros_like(first)
    rows = [0.5 * last, 0.5 * stress_right, -0.5 * stress_left, -0.5 * first]
    rows = jnp.concatenate([*rows, last, first, nothing, nothing], axis=0)
    size = rows.shape[1] // chunks
    pieces = [rows[:, place * size : (place + 1) * size] for place in range(chunks)]
    pieces.append(jnp.zeros((size - 8 * chunks, size), rows.dtype))
    return jnp.concatenate(pieces, axis=0).T


def strike_edge(target, base, velocity, rigidity, stress_x, inner, sign):
    target[base : base + 16] = velocity
    target[base + 16 : base + 32] = rigidity
    target[base + 32 : base + 48] = stress_x + (sign * courant * 0.5) * rigidity * inner


def deal(total, core, own, surface):
    nodes = total.shape[0] // 5
    for place, index in enumerate((0, 2, 4)):
        own[surface, place * nodes : (place + 1) * nodes] = total[
            index * nodes : (index + 1) * nodes
        ]
    base = surface * 2 * nodes
    core[base : base + nodes] = total[nodes : 2 * nodes]
    core[base + nodes : base + 2 * nodes] = total[3 * nodes : 4 * nodes]


def first_kernel(*refs):
    (velocity, stress, rigidity, cone, history, kernel), rest = refs[:6], refs[6:11]
    core, own, later, lead, edges, edges_sent, speed, tension, rigid = refs[11:20]
    rest_held = refs[20:25]
    limits, past, matrix, slab_sems, part_sems, rest_sems = refs[25:]
    surfaces, rows, columns = kernel.shape
    nodes, ny, width = velocity.shape
    offsets = rows // nodes
    reach = (offsets - 1) // 2
    parts = columns // CHUNK_COLUMNS

    slab = [
        pltpu.make_async_copy(source, target, slab_sems.at[place])
        for place, (source, target) in enumerate(
            ((cone, limits), (velocity, speed), (rigidity, rigid), (stress, tension))
        )
    ]
    piece = columns // SPLIT
    fetches = []
    for surface in range(surfaces):
        for half in range(SPLIT):
            place, span = len(fetches), pl.ds(half * piece, piece)
            fetches.append(
                (
                    pltpu.make_async_copy(
                        history.at[surface, span], past.at[surface, span], part_sems.at[0, place]
                    ),
                    pltpu.make_async_copy(
                        kernel.at[surface, :, span],
                        matrix.at[surface, :, span],
                        part_sems.at[1, place],
                    ),
                )
            )
    others = [
        pltpu.make_async_copy(source, target.at[pl.ds(0, source.shape[0])], rest_sems.at[place])
        for place, (source, target) in enumerate(zip(rest, rest_held))
    ]
    following = {0: (*fetches[3], *slab[1:]), 1: others}
    for copy in (slab[0], *fetches[0], *fetches[1]):
        copy.start()
    slab[0].wait()
    for copy in fetches[2]:
        copy.start()

    block = lax.axis_index(GX)
    blocks = cone.shape[3]
    lag = lax.div(lane_of((1, CHUNK_COLUMNS)), nodes)
    order = [(surface, part) for surface in range(surfaces) for part in range(parts)]
    for surface, part in order:
        at = part * CHUNK_COLUMNS
        if at % piece == 0:
            place = surface * SPLIT + at // piece
            for copy in fetches[place]:
                copy.wait()
            for copy in following.get(place, ()):
                copy.start()
        if (surface, part) == order[-1]:
            for copy in slab[1:]:
                copy.wait()
            cells = [slice(at, at + CHUNK) for at in range(0, nodes, CHUNK)]
            depth_edges(edges, edges_sent, [(speed[c], tension[1, c], rigid[c]) for c in cells])
            base = 4 * nodes
            strike_edge(core, base, speed[0], rigid[0], tension[0, 0], speed[1], 1.0)
            strike_edge(
                core,
                base + 48,
                speed[nodes - 1],
                rigid[nodes - 1],
                tension[0, nodes - 1],
                speed[nodes - 2],
                -1.0,
            )
        masked = []
        for index in range(offsets):
            target = jnp.clip(block + (index - reach), 0, blocks - 1)
            first = limits[surface, index, 0, target]
            last = limits[surface, index, 1, target]
            now = lag + at // nodes
            keep = jnp.where((now >= first) & (now < last), 1.0, 0.0).astype(jnp.bfloat16)
            masked.append(
                matrix[surface, index * nodes : (index + 1) * nodes, at : at + CHUNK_COLUMNS]
                * keep
            )
        kept = jnp.concatenate(masked, axis=0)
        now = past[surface, at : at + CHUNK_COLUMNS]
        if part:
            before = past[surface, at - nodes : at + CHUNK_COLUMNS - nodes]
        else:
            before = jnp.concatenate(
                [jnp.zeros((nodes, width), now.dtype), now[: CHUNK_COLUMNS - nodes]], axis=0
            )
            lead[surface] = kept[:, :nodes]
        both = jnp.concatenate([now, before], axis=1)
        product = jnp.dot(kept, both, preferred_element_type=jnp.float32)
        total = total + product if part else product
        if part == parts - 1:
            later[surface] = total[:, width:]
            deal(total[:, :width], core, own, surface)
    for copy in others:
        copy.wait()


def pinned(x):
    return pltpu.with_memory_space_constraint(x, pltpu.HBM)


def first_call(velocity, stress, rigidity, cone, history, kernel, *rest):
    surfaces, rows, columns = kernel.shape
    nodes, ny, width = velocity.shape
    f32 = jnp.float32
    return pl.pallas_call(
        first_kernel,
        in_specs=[pl.BlockSpec(memory_space=pltpu.HBM)] * (6 + len(rest)),
        out_specs=[pl.BlockSpec(memory_space=pltpu.VMEM)] * (9 + len(rest)),
        out_shape=[
            jax.ShapeDtypeStruct((4 * nodes + 96, width), f32),
            jax.ShapeDtypeStruct((surfaces, 3 * nodes, width), f32),
            jax.ShapeDtypeStruct((surfaces, rows, width), f32),
            jax.ShapeDtypeStruct((surfaces, rows, nodes), jnp.bfloat16),
            jax.ShapeDtypeStruct((8, nodes * ny), f32),
            jax.ShapeDtypeStruct((nodes, width), jnp.bfloat16),
        ]
        + [
            jax.ShapeDtypeStruct(shape, f32)
            for shape in (velocity.shape, stress.shape, rigidity.shape, (nodes * ny, width))
        ]
        + [jax.ShapeDtypeStruct(x.shape, f32) for x in rest[1:]],
        scratch_shapes=[
            pltpu.SMEM(cone.shape, jnp.int32),
            pltpu.VMEM(history.shape, history.dtype),
            pltpu.VMEM(kernel.shape, kernel.dtype),
            pltpu.SemaphoreType.DMA((4,)),
            pltpu.SemaphoreType.DMA((2, surfaces * SPLIT)),
            pltpu.SemaphoreType.DMA((len(rest),)),
        ],
        compiler_params=pltpu.CompilerParams(vmem_limit_bytes=FIRST_LIMIT),
    )(*(pinned(x) for x in (velocity, stress, rigidity, cone, history, kernel, *rest)))


def packed_into(target, parts):
    base, powers = 0, []
    for part in parts:
        size = part.shape[0]
        most = jnp.max(jnp.abs(part), axis=0, keepdims=True)
        power = jnp.ceil(jnp.log2(jnp.maximum(most, 2.0**-100)))
        powers.append(power)
        target[base : base + size] = jnp.round(part * jnp.exp2(14.0 - power)).astype(jnp.int16)
        base += size
    powers.append(jnp.zeros((16 - len(powers), powers[0].shape[1]), jnp.float32))
    target[base : base + 16] = jnp.concatenate(powers, axis=0).astype(jnp.int16)
    if target.shape[0] > base + 16:
        target[base + 16 :] = jnp.zeros_like(target[base + 16 :])


def unpacked(source, nodes):
    sizes = (nodes, nodes, 16, 16, 16)
    base, parts = 0, []
    last = sum(sizes)
    scales = jnp.exp2(source[last : last + 16].astype(jnp.float32) - 14.0)
    for place, size in enumerate(sizes):
        part = source[base : base + size].astype(jnp.float32)
        parts.append(part * scales[place : place + 1])
        base += size
    return parts


def relay_kernel(near, received, own, *refs):
    target = refs[-1]
    even, chip_even, _ = parities()
    to_right = chip_even if near else jnp.logical_not(chip_even)
    nodes = own.shape[1] // 3
    parts = []
    for surface in range(2):
        base = surface * 2 * nodes
        from_left = received[base : base + nodes]
        from_right = received[base + nodes : base + 2 * nodes]
        nothing = jnp.zeros_like(from_left)
        left = own[surface, :nodes] + lax.select(even, nothing, from_left)
        right = own[surface, 2 * nodes :] + lax.select(even, from_right, nothing)
        parts.append(lax.select(to_right, right, left))
    base = 4 * nodes
    halo = lax.select(to_right, received[base + 48 :], received[base : base + 48])
    packed_into(target, parts + [halo[at : at + 16] for at in (0, 16, 32)])


def relay_call(near, received, own, *after):
    nodes, width = own.shape[1] // 3, own.shape[2]
    rows = 2 * nodes + 64 + (0 if near else SPARE)
    return pl.pallas_call(
        functools.partial(relay_kernel, near),
        out_shape=jax.ShapeDtypeStruct((rows, width), jnp.int16),
        compiler_params=pltpu.CompilerParams(vmem_limit_bytes=4 * MIB),
    )(received, own, *after)


def beside(ref, at):
    nodes = ref.shape[0]
    up = ref[at + 1 : min(at + CHUNK + 1, nodes)]
    down = ref[max(at - 1, 0) : at + CHUNK - 1]
    nothing = jnp.zeros((1, *ref.shape[1:]), jnp.float32)
    if at + CHUNK == nodes:
        up = jnp.concatenate([up, nothing], axis=0)
    if at == 0:
        down = jnp.concatenate([nothing, down], axis=0)
    return up, down


def inner_kernel(last, *refs):
    velocity, stress, stress_y, rigidity, buoyancy = refs[:5]
    if last:
        stiffness, moved, stress_new, faces_new = refs[5:]
    else:
        moved, stress_new, faces_new, stiffness = refs[5:]
    nodes, ny, width = velocity.shape
    scale = courant * 0.5
    shape = (CHUNK, ny, width)
    lane = lane_of(shape)
    level = lax.broadcasted_iota(jnp.int32, shape, 1)

    def across(value):
        after = jnp.where(lane == width - 1, 0.0, turned(value, -1))
        before = jnp.where(lane == 0, 0.0, turned(value, 1))
        return after - before

    def stresses(at):
        cells = slice(at, at + CHUNK)
        here, rigid = velocity[cells], rigidity[cells]
        up, down = beside(velocity, at)
        stress_new[0, cells] = stress[0, cells] + scale * rigid * (up - down)
        stress_z = stress[1, cells] + scale * rigid * across(here)
        stress_new[1, cells] = stress_z
        if last:
            faces, stiff = stress_y[cells], stiffness[cells]
        else:
            faces = jnp.stack(
                [stress_y[pl.ds(at + r, ny, stride=nodes), :] for r in range(CHUNK)]
            )
            stiff = courant * (0.5 * (pltpu.roll(rigid, ny - 1, 1) + rigid))
            stiffness[cells] = stiff
        trial = faces + stiff * (pltpu.roll(here, ny - 1, 1) - here)
        trial = jnp.where(level == ny - 1, 0.0, trial)
        if last:
            for r in range(CHUNK):
                faces_new[pl.ds(at + r, ny, stride=nodes), :] = trial[r]
        else:
            faces_new[cells] = trial
        return 0.5 * across(stress_z) + trial - pltpu.roll(trial, 1, 1)

    def velocities(at, partial):
        cells = slice(at, at + CHUNK)
        up, down = beside(stress_new.at[0], at)
        moved[cells] = velocity[cells] + courant * buoyancy[cells] * (0.5 * (up - down) + partial)

    partial = stresses(0)
    for at in range(CHUNK, nodes, CHUNK):
        following = stresses(at)
        velocities(at - CHUNK, partial)
        partial = following
    velocities(nodes - CHUNK, partial)


def inner_call(last, *args):
    nodes, ny, width = args[0].shape
    shapes = [(nodes, ny, width), (2, nodes, ny, width)]
    shapes += [(nodes * ny, width)] if last else [(nodes, ny, width)] * 2
    return pl.pallas_call(
        functools.partial(inner_kernel, last),
        out_shape=[jax.ShapeDtypeStruct(shape, jnp.float32) for shape in shapes],
        out_specs=[pl.BlockSpec(memory_space=pltpu.VMEM)] * len(shapes),
        compiler_params=pltpu.CompilerParams(vmem_limit_bytes=8 * MIB),
    )(*args)


def step_kernel(last, *refs):
    (moved, stress, faces, velocity, rigidity, buoyancy) = refs[:6]
    (sigma_star, sigma_zero, friction) = refs[6:9]
    (received, near, far, depth_own, depth_near, depth_far, own) = refs[9:16]
    refs = refs[16:]
    nodes, ny, width = velocity.shape
    chunks = nodes // CHUNK
    fault = ny // 2 - 1
    scale = courant * 0.5
    copies = []
    if last:
        results, (velocity_new, shear, tips, broken, state_new, bounds), sems = (
            refs[:5],
            refs[5:11],
            refs[11],
        )

        def send(source, target):
            copies.append(pltpu.make_async_copy(source, target, sems.at[len(copies)]))
            copies[-1].start()

        inner = pl.ds(1, nodes - 2)
        send(stress.at[0, inner], results[1].at[0, inner])
        base = fault * nodes
        send(faces.at[pl.ds(0, base)], results[2].at[pl.ds(0, base)])
        above = pl.ds(base + nodes, (ny - 2 - fault) * nodes)
        send(faces.at[above], results[2].at[above])
    else:
        later, lead = refs[:2]
        velocity_new, stress_new, faces_new, state_new, core, own_new, edges = refs[2:9]
        edges_sent = refs[9]
        shear = stress_new.at[1]
    even, chip_even, _ = parities()

    def level_of(ref, y):
        return ref.reshape(nodes * ny, width)[pl.ds(y, nodes, stride=ny), :]

    near_parts, far_parts = unpacked(near, nodes), unpacked(far, nodes)
    traction = []
    for surface in range(2):
        base = surface * 2 * nodes
        mate = lax.select(
            even, received[base : base + nodes], received[base + nodes : base + 2 * nodes]
        )
        traction.append(
            own[surface, nodes : 2 * nodes] + mate + (near_parts[surface] + far_parts[surface])
        )

    near_halo, far_halo = (jnp.concatenate(x[2:], axis=0) for x in (near_parts, far_parts))
    left = lax.select(
        even, lax.select(chip_even, far_halo, near_halo), received[4 * nodes + 48 :]
    )
    right = lax.select(
        even, received[4 * nodes : 4 * nodes + 48], lax.select(chip_even, near_halo, far_halo)
    )
    stress_left = left[32:] + scale * left[16:32] * velocity[0]
    stress_right = right[32:] - scale * right[16:32] * velocity[nodes - 1]
    added_left = -scale * rigidity[0] * left[:16]
    added_right = scale * rigidity[nodes - 1] * right[:16]

    shape = (CHUNK, ny, width)
    sides = depth_sides(depth_own[...], depth_near[...], depth_far[...], chunks).reshape(shape)
    lane = lane_of(shape)
    edge = (lane == 0) | (lane == width - 1)
    margin = (lane < 2) | (lane >= width - 2)

    for at in range(0, nodes, CHUNK):
        cells = slice(at, at + CHUNK)
        place = 8 * (at // CHUNK)
        extra = jnp.where(margin, turned(sides, -(place + 2)), 0.0)
        velocity_new[cells] = moved[cells] + courant * buoyancy[cells] * extra
        extra = jnp.where(edge, turned(sides, -(place + 5)), 0.0)
        shear[cells] = stress[1, cells] + extra
        if last and (at + CHUNK) % (nodes // 2) == 0:
            half = pl.ds(at + CHUNK - nodes // 2, nodes // 2)
            send(shear.at[half], results[1].at[1, half])
        if not last:
            stress_new[0, cells] = stress[0, cells]
            faces_new[cells] = faces[cells]

    first_row, last_row = stress[0, 0] + added_left, stress[0, nodes - 1] + added_right
    if last:
        tips[0], tips[1] = first_row, last_row
        send(tips.at[0], results[1].at[0, 0])
        send(tips.at[1], results[1].at[0, nodes - 1])
    else:
        stress_new[0, 0], stress_new[0, nodes - 1] = first_row, last_row

    row = lax.broadcasted_iota(jnp.int32, (nodes, width), 0)
    lower, upper = slice(fault, fault + 1), slice(fault + 1, fault + 2)
    across = level_of(stress.at[0], fault + 1) - level_of(stress.at[0], fault)
    across = across + jnp.where(row == 0, added_left[upper] - added_left[lower], 0.0)
    across = across + jnp.where(row == nodes - 1, added_right[upper] - added_right[lower], 0.0)
    slip_rate = level_of(velocity, fault + 1) - level_of(velocity, fault)
    normal = sigma_zero[...] + bimaterial * jnp.tanh(across)
    state = normal + (sigma_star[...] - normal) * jnp.exp(
        -(jnp.abs(slip_rate) + slip_ref) * decay_rate
    )
    state_new[...] = state
    strength = friction[...] * state
    trial = faces[fault * nodes : (fault + 1) * nodes] if last else level_of(faces, fault)
    clipped = jnp.clip(trial, -strength, strength)
    bottom = traction[0] + impedance * level_of(velocity, 0)
    top = traction[1] - impedance * level_of(velocity, ny - 1)
    if last:
        broken[...] = clipped
        bounds[0], bounds[1] = bottom, top
        send(broken, results[2].at[pl.ds(fault * nodes, nodes)])
        send(state_new, results[3])
        send(bounds, results[4])
    else:
        faces_new.reshape(nodes * ny, width)[pl.ds(fault, nodes, stride=ny), :] = clipped

    flat = velocity_new.reshape(nodes * ny, width)
    for y, change in (
        (fault, clipped - trial),
        (fault + 1, trial - clipped),
        (0, -bottom),
        (ny - 1, top),
    ):
        at = pl.ds(y, nodes, stride=ny)
        flat[at, :] = flat[at, :] + courant * level_of(buoyancy, y) * change
    for x, change in (
        (0, -stress_left),
        (1, -added_left),
        (nodes - 2, added_right),
        (nodes - 1, stress_right),
    ):
        velocity_new[x] = velocity_new[x] + (0.5 * courant) * buoyancy[x] * change

    if last:
        send(velocity_new, results[0])
        for copy in copies:
            copy.wait()
        return

    for surface in range(2):
        fresh = level_of(velocity_new, surface * (ny - 1)).astype(jnp.bfloat16)
        total = later[surface] + jnp.dot(
            lead[surface], fresh, preferred_element_type=jnp.float32
        )
        deal(total, core, own_new, surface)
    strike_edge(
        core, 4 * nodes, velocity_new[0], rigidity[0], stress_new[0, 0], velocity_new[1], 1.0
    )
    strike_edge(
        core,
        4 * nodes + 48,
        velocity_new[nodes - 1],
        rigidity[nodes - 1],
        stress_new[0, nodes - 1],
        velocity_new[nodes - 2],
        -1.0,
    )
    cells = [slice(at, at + CHUNK) for at in range(0, nodes, CHUNK)]
    depth_edges(edges, edges_sent, [(velocity_new[c], stress_new[1, c], rigidity[c]) for c in cells])


def step_call(last, *args):
    nodes, ny, width = args[0].shape
    f32 = jnp.float32
    shapes = [(nodes, ny, width), (2, nodes, ny, width)]
    if last:
        shapes += [(nodes * (ny - 1), width), (nodes, width), (2, nodes, width)]
        held = [(nodes, ny, width)] * 2 + [(2, ny, width), (nodes, width), *shapes[3:]]
        scratch = [pltpu.VMEM(shape, f32) for shape in held]
        scratch += [pltpu.SemaphoreType.DMA((11,))]
        space = pltpu.HBM
    else:
        shapes += [
            (nodes, ny, width),
            (nodes, width),
            (4 * nodes + 96, width),
            (2, 3 * nodes, width),
            (8, nodes * ny),
        ]
        scratch, space = [], pltpu.VMEM
    out_shape = [jax.ShapeDtypeStruct(shape, f32) for shape in shapes]
    if not last:
        out_shape.append(jax.ShapeDtypeStruct((nodes, width), jnp.bfloat16))
    return pl.pallas_call(
        functools.partial(step_kernel, last),
        out_shape=out_shape,
        out_specs=[pl.BlockSpec(memory_space=space)] * len(out_shape),
        scratch_shapes=scratch,
        compiler_params=pltpu.CompilerParams(vmem_limit_bytes=16 * MIB),
    )(*args)


def exchange(core, own, edges, edges_sent):
    received = lax.ppermute(core, GX, swap_pairs(GX, 1, 0))
    depth_near = lax.ppermute(edges_sent, GZ, swap_pairs(GZ, 1, 0))
    far = lax.ppermute(relay_call(False, received, own), GX, swap_pairs(GX, 2, 2))
    near = relay_call(True, received, own, depth_near)
    near = lax.ppermute(near, GX, swap_pairs(GX, 2, 0))
    depth_far = lax.ppermute(depth_near, GZ, onward_pairs(GZ))
    return received, near, far, edges, depth_near, depth_far


def local(
    velocity,
    stress_xz,
    stress_y,
    rigidity,
    buoyancy,
    sigma_star,
    sigma_zero,
    friction,
    history,
    kernel,
    cone,
):
    surfaces, lags, nodes, width = history.shape
    faces = stress_y.shape[1]
    past = history.reshape(surfaces, lags * nodes, width)
    matrix = kernel.reshape(surfaces, -1, kernel.shape[3])
    turned_cone = jnp.transpose(cone, (0, 2, 3, 1))
    face_rows = jnp.transpose(stress_y, (1, 0, 2)).reshape(faces * nodes, width)
    core, own, later, lead, edges, sent, velocity, stress_xz, rigidity, *rest = first_call(
        velocity,
        stress_xz,
        rigidity,
        turned_cone,
        past,
        matrix,
        face_rows,
        buoyancy,
        sigma_star,
        sigma_zero,
        friction,
    )
    face_rows, buoyancy, sigma_star, sigma_zero, friction = rest
    *inner, stiffness = inner_call(False, velocity, stress_xz, face_rows, rigidity, buoyancy)
    velocity, stress_xz, stress_y, state, core, own, edges, sent = step_call(
        False,
        *inner,
        velocity,
        rigidity,
        buoyancy,
        sigma_star,
        sigma_zero,
        friction,
        *exchange(core, own, edges, sent),
        own,
        later,
        lead,
    )
    inner = inner_call(True, velocity, stress_xz, stress_y, rigidity, buoyancy, stiffness)
    velocity, stress_xz, face_rows, state, bounds = step_call(
        True,
        *inner,
        velocity,
        rigidity,
        buoyancy,
        state,
        sigma_zero,
        friction,
        *exchange(core, own, edges, sent),
        own,
    )
    stress_y = jnp.transpose(face_rows.reshape(faces, nodes, width), (1, 0, 2))
    return velocity, stress_xz, stress_y, state, bounds


def solution(mesh):
    in_specs = (
        P("gx", None, "gz"),
        P(None, "gx", None, "gz"),
        P("gx", None, "gz"),
        P("gx", None, "gz"),
        P("gx", None, "gz"),
        P("gx", "gz"),
        P("gx", "gz"),
        P("gx", "gz"),
        P(None, None, "gx", "gz"),
        P(),
        P(),
    )
    out_specs = (
        P("gx", None, "gz"),
        P(None, "gx", None, "gz"),
        P("gx", None, "gz"),
        P("gx", "gz"),
        P(None, "gx", "gz"),
    )
    return jax.shard_map(
        local, mesh=mesh, in_specs=in_specs, out_specs=tuple(out_specs), check_vma=False
    )
```

```python
import functools

import jax
import jax.numpy as jnp
from jax import lax
from jax.experimental import pallas as pl
from jax.experimental.pallas import tpu as pltpu
from jax.sharding import PartitionSpec as P

courant = 0.25
bimaterial = 0.5
slip_ref = 0.2
decay_rate = 0.5
impedance = 0.5

GX, GZ = "gx", "gz"
CHUNK = 8
CHUNK_COLUMNS = 1024
SPLIT = 2
SPARE = 16
MIB = 2**20
FIRST_LIMIT = 12 * MIB


def swap_pairs(axis, distance, phase):
    size, pairs = lax.axis_size(axis), []
    for i in range(size):
        partner = i + distance if (i - phase) % (2 * distance) < distance else i - distance
        if 0 <= partner < size:
            pairs.append((i, partner))
    return pairs


def onward_pairs(axis):
    size, pairs = lax.axis_size(axis), []
    for i in range(size):
        partner = i + 2 if i % 2 == 0 else i - 2
        if 0 <= partner < size:
            pairs.append((i, partner))
    return pairs


def parities():
    block = lax.axis_index(GX)
    even = lax.rem(block, 2) == 0
    chip_even = lax.rem(lax.div(block, 2), 2) == 0
    depth_even = lax.rem(lax.axis_index(GZ), 2) == 0
    return even, chip_even, depth_even


def lane_of(shape):
    return lax.broadcasted_iota(jnp.int32, shape, len(shape) - 1)


def turned(value, shift):
    return pltpu.roll(value, shift % value.shape[-1], value.ndim - 1)


def depth_edges(edges, edges_sent, cells):
    packed, group = None, 8
    for place, (velocity, stress_z, rigidity) in enumerate(cells):
        base = place * group
        lane = lane_of(velocity.shape)
        if packed is None:
            packed = jnp.zeros(velocity.shape, velocity.dtype)
        packed = jnp.where(
            lane < base,
            packed,
            jnp.where(
                lane < base + 4,
                turned(velocity, base + 2),
                jnp.where(lane < base + 6, turned(stress_z, base + 5), turned(rigidity, base + 7)),
            ),
        )
    size = packed.shape[0] * packed.shape[1]
    rows = packed.reshape(size, -1).T
    for place in range(len(cells)):
        edges[:, place * size : (place + 1) * size] = rows[place * group : (place + 1) * group]
    edges_sent[...] = rows[: edges_sent.shape[0]].astype(edges_sent.dtype)


def depth_sides(own, near, far, chunks):
    _, _, depth_even = parities()
    near, far = (
        jnp.concatenate([x[at : at + 8] for at in range(0, x.shape[0], 8)], axis=1)
        for x in (near.astype(jnp.float32), far.astype(jnp.float32))
    )
    left = lax.select(depth_even, far, near)
    right = lax.select(depth_even, near, far)
    scale = courant * 0.5
    stress_left = left[4:5] + scale * left[6:7] * (own[2:3] - left[0:1])
    stress_right = right[5:6] + scale * right[7:8] * (right[3:4] - own[1:2])
    first = -scale * own[7:8] * left[1:2]
    last = scale * own[6:7] * right[2:3]
    nothing = jnp.zeros_like(first)
    rows = [0.5 * last, 0.5 * stress_right, -0.5 * stress_left, -0.5 * first]
    rows = jnp.concatenate([*rows, last, first, nothing, nothing], axis=0)
    size = rows.shape[1] // chunks
    pieces = [rows[:, place * size : (place + 1) * size] for place in range(chunks)]
    pieces.append(jnp.zeros((size - 8 * chunks, size), rows.dtype))
    return jnp.concatenate(pieces, axis=0).T


def strike_edge(target, base, velocity, rigidity, stress_x, inner, sign):
    target[base : base + 16] = velocity
    target[base + 16 : base + 32] = rigidity
    target[base + 32 : base + 48] = stress_x + (sign * courant * 0.5) * rigidity * inner


def deal(total, core, own, surface):
    nodes = total.shape[0] // 5
    for place, index in enumerate((0, 2, 4)):
        own[surface, place * nodes : (place + 1) * nodes] = total[
            index * nodes : (index + 1) * nodes
        ]
    base = surface * 2 * nodes
    core[base : base + nodes] = total[nodes : 2 * nodes]
    core[base + nodes : base + 2 * nodes] = total[3 * nodes : 4 * nodes]


def first_kernel(*refs):
    (velocity, stress, rigidity, cone, history, kernel), rest = refs[:6], refs[6:11]
    core, own, later, lead, edges, edges_sent, speed, tension, rigid = refs[11:20]
    rest_held = refs[20:25]
    limits, past, matrix, slab_sems, part_sems, rest_sems = refs[25:]
    surfaces, rows, columns = kernel.shape
    nodes, ny, width = velocity.shape
    offsets = rows // nodes
    reach = (offsets - 1) // 2
    parts = columns // CHUNK_COLUMNS

    slab = [
        pltpu.make_async_copy(source, target, slab_sems.at[place])
        for place, (source, target) in enumerate(
            ((cone, limits), (velocity, speed), (rigidity, rigid), (stress, tension))
        )
    ]
    piece = columns // SPLIT
    fetches = []
    for surface in range(surfaces):
        for half in range(SPLIT):
            place, span = len(fetches), pl.ds(half * piece, piece)
            fetches.append(
                (
                    pltpu.make_async_copy(
                        history.at[surface, span], past.at[surface, span], part_sems.at[0, place]
                    ),
                    pltpu.make_async_copy(
                        kernel.at[surface, :, span],
                        matrix.at[surface, :, span],
                        part_sems.at[1, place],
                    ),
                )
            )
    others = [
        pltpu.make_async_copy(source, target.at[pl.ds(0, source.shape[0])], rest_sems.at[place])
        for place, (source, target) in enumerate(zip(rest, rest_held))
    ]
    following = {0: (*fetches[3], *slab[1:]), 1: others}
    for copy in (slab[0], *fetches[0], *fetches[1]):
        copy.start()
    slab[0].wait()
    for copy in fetches[2]:
        copy.start()

    block = lax.axis_index(GX)
    blocks = cone.shape[3]
    lag = lax.div(lane_of((1, CHUNK_COLUMNS)), nodes)
    order = [(surface, part) for surface in range(surfaces) for part in range(parts)]
    for surface, part in order:
        at = part * CHUNK_COLUMNS
        if at % piece == 0:
            place = surface * SPLIT + at // piece
            for copy in fetches[place]:
                copy.wait()
            for copy in following.get(place, ()):
                copy.start()
        if (surface, part) == order[-1]:
            for copy in slab[1:]:
                copy.wait()
            cells = [slice(at, at + CHUNK) for at in range(0, nodes, CHUNK)]
            depth_edges(edges, edges_sent, [(speed[c], tension[1, c], rigid[c]) for c in cells])
            base = 4 * nodes
            strike_edge(core, base, speed[0], rigid[0], tension[0, 0], speed[1], 1.0)
            strike_edge(
                core,
                base + 48,
                speed[nodes - 1],
                rigid[nodes - 1],
                tension[0, nodes - 1],
                speed[nodes - 2],
                -1.0,
            )
        masked = []
        for index in range(offsets):
            target = jnp.clip(block + (index - reach), 0, blocks - 1)
            first = limits[surface, index, 0, target]
            last = limits[surface, index, 1, target]
            now = lag + at // nodes
            keep = jnp.where((now >= first) & (now < last), 1.0, 0.0).astype(jnp.bfloat16)
            masked.append(
                matrix[surface, index * nodes : (index + 1) * nodes, at : at + CHUNK_COLUMNS]
                * keep
            )
        kept = jnp.concatenate(masked, axis=0)
        now = past[surface, at : at + CHUNK_COLUMNS]
        if part:
            before = past[surface, at - nodes : at + CHUNK_COLUMNS - nodes]
        else:
            before = jnp.concatenate(
                [jnp.zeros((nodes, width), now.dtype), now[: CHUNK_COLUMNS - nodes]], axis=0
            )
            lead[surface] = kept[:, :nodes]
        both = jnp.concatenate([now, before], axis=1)
        product = jnp.dot(kept, both, preferred_element_type=jnp.float32)
        total = total + product if part else product
        if part == parts - 1:
            later[surface] = total[:, width:]
            deal(total[:, :width], core, own, surface)
    for copy in others:
        copy.wait()


def pinned(x):
    return pltpu.with_memory_space_constraint(x, pltpu.HBM)


def first_call(velocity, stress, rigidity, cone, history, kernel, *rest):
    surfaces, rows, columns = kernel.shape
    nodes, ny, width = velocity.shape
    f32 = jnp.float32
    return pl.pallas_call(
        first_kernel,
        in_specs=[pl.BlockSpec(memory_space=pltpu.HBM)] * (6 + len(rest)),
        out_specs=[pl.BlockSpec(memory_space=pltpu.VMEM)] * (9 + len(rest)),
        out_shape=[
            jax.ShapeDtypeStruct((4 * nodes + 96, width), f32),
            jax.ShapeDtypeStruct((surfaces, 3 * nodes, width), f32),
            jax.ShapeDtypeStruct((surfaces, rows, width), f32),
            jax.ShapeDtypeStruct((surfaces, rows, nodes), jnp.bfloat16),
            jax.ShapeDtypeStruct((8, nodes * ny), f32),
            jax.ShapeDtypeStruct((nodes, width), jnp.bfloat16),
        ]
        + [
            jax.ShapeDtypeStruct(shape, f32)
            for shape in (velocity.shape, stress.shape, rigidity.shape, (nodes * ny, width))
        ]
        + [jax.ShapeDtypeStruct(x.shape, f32) for x in rest[1:]],
        scratch_shapes=[
            pltpu.SMEM(cone.shape, jnp.int32),
            pltpu.VMEM(history.shape, history.dtype),
            pltpu.VMEM(kernel.shape, kernel.dtype),
            pltpu.SemaphoreType.DMA((4,)),
            pltpu.SemaphoreType.DMA((2, surfaces * SPLIT)),
            pltpu.SemaphoreType.DMA((len(rest),)),
        ],
        compiler_params=pltpu.CompilerParams(vmem_limit_bytes=FIRST_LIMIT),
    )(*(pinned(x) for x in (velocity, stress, rigidity, cone, history, kernel, *rest)))


def packed_into(target, parts):
    base, powers = 0, []
    for part in parts:
        size = part.shape[0]
        most = jnp.max(jnp.abs(part), axis=0, keepdims=True)
        power = jnp.ceil(jnp.log2(jnp.maximum(most, 2.0**-100)))
        powers.append(power)
        target[base : base + size] = jnp.round(part * jnp.exp2(14.0 - power)).astype(jnp.int16)
        base += size
    powers.append(jnp.zeros((16 - len(powers), powers[0].shape[1]), jnp.float32))
    target[base : base + 16] = jnp.concatenate(powers, axis=0).astype(jnp.int16)
    if target.shape[0] > base + 16:
        target[base + 16 :] = jnp.zeros_like(target[base + 16 :])


def unpacked(source, nodes):
    sizes = (nodes, nodes, 16, 16, 16)
    base, parts = 0, []
    last = sum(sizes)
    scales = jnp.exp2(source[last : last + 16].astype(jnp.float32) - 14.0)
    for place, size in enumerate(sizes):
        part = source[base : base + size].astype(jnp.float32)
        parts.append(part * scales[place : place + 1])
        base += size
    return parts


def relay_kernel(near, received, own, *refs):
    target = refs[-1]
    even, chip_even, _ = parities()
    to_right = chip_even if near else jnp.logical_not(chip_even)
    nodes = own.shape[1] // 3
    parts = []
    for surface in range(2):
        base = surface * 2 * nodes
        from_left = received[base : base + nodes]
        from_right = received[base + nodes : base + 2 * nodes]
        nothing = jnp.zeros_like(from_left)
        left = own[surface, :nodes] + lax.select(even, nothing, from_left)
        right = own[surface, 2 * nodes :] + lax.select(even, from_right, nothing)
        parts.append(lax.select(to_right, right, left))
    base = 4 * nodes
    halo = lax.select(to_right, received[base + 48 :], received[base : base + 48])
    packed_into(target, parts + [halo[at : at + 16] for at in (0, 16, 32)])


def relay_call(near, received, own, *after):
    nodes, width = own.shape[1] // 3, own.shape[2]
    rows = 2 * nodes + 64 + (0 if near else SPARE)
    return pl.pallas_call(
        functools.partial(relay_kernel, near),
        out_shape=jax.ShapeDtypeStruct((rows, width), jnp.int16),
        compiler_params=pltpu.CompilerParams(vmem_limit_bytes=4 * MIB),
    )(received, own, *after)


def beside(ref, at):
    nodes = ref.shape[0]
    up = ref[at + 1 : min(at + CHUNK + 1, nodes)]
    down = ref[max(at - 1, 0) : at + CHUNK - 1]
    nothing = jnp.zeros((1, *ref.shape[1:]), jnp.float32)
    if at + CHUNK == nodes:
        up = jnp.concatenate([up, nothing], axis=0)
    if at == 0:
        down = jnp.concatenate([nothing, down], axis=0)
    return up, down


def inner_kernel(last, *refs):
    velocity, stress, stress_y, rigidity, buoyancy = refs[:5]
    if last:
        stiffness, moved, stress_new, faces_new = refs[5:]
    else:
        moved, stress_new, faces_new, stiffness = refs[5:]
    nodes, ny, width = velocity.shape
    scale = courant * 0.5
    shape = (CHUNK, ny, width)
    lane = lane_of(shape)
    level = lax.broadcasted_iota(jnp.int32, shape, 1)

    def across(value):
        after = jnp.where(lane == width - 1, 0.0, turned(value, -1))
        before = jnp.where(lane == 0, 0.0, turned(value, 1))
        return after - before

    def stresses(at):
        cells = slice(at, at + CHUNK)
        here, rigid = velocity[cells], rigidity[cells]
        up, down = beside(velocity, at)
        stress_new[0, cells] = stress[0, cells] + scale * rigid * (up - down)
        stress_z = stress[1, cells] + scale * rigid * across(here)
        stress_new[1, cells] = stress_z
        if last:
            faces, stiff = stress_y[cells], stiffness[cells]
        else:
            faces = jnp.stack(
                [stress_y[pl.ds(at + r, ny, stride=nodes), :] for r in range(CHUNK)]
            )
            stiff = courant * (0.5 * (pltpu.roll(rigid, ny - 1, 1) + rigid))
            stiffness[cells] = stiff
        trial = faces + stiff * (pltpu.roll(here, ny - 1, 1) - here)
        trial = jnp.where(level == ny - 1, 0.0, trial)
        if last:
            for r in range(CHUNK):
                faces_new[pl.ds(at + r, ny, stride=nodes), :] = trial[r]
        else:
            faces_new[cells] = trial
        return 0.5 * across(stress_z) + trial - pltpu.roll(trial, 1, 1)

    def velocities(at, partial):
        cells = slice(at, at + CHUNK)
        up, down = beside(stress_new.at[0], at)
        moved[cells] = velocity[cells] + courant * buoyancy[cells] * (0.5 * (up - down) + partial)

    partial = stresses(0)
    for at in range(CHUNK, nodes, CHUNK):
        following = stresses(at)
        velocities(at - CHUNK, partial)
        partial = following
    velocities(nodes - CHUNK, partial)


def inner_call(last, *args):
    nodes, ny, width = args[0].shape
    shapes = [(nodes, ny, width), (2, nodes, ny, width)]
    shapes += [(nodes * ny, width)] if last else [(nodes, ny, width)] * 2
    return pl.pallas_call(
        functools.partial(inner_kernel, last),
        out_shape=[jax.ShapeDtypeStruct(shape, jnp.float32) for shape in shapes],
        out_specs=[pl.BlockSpec(memory_space=pltpu.VMEM)] * len(shapes),
        compiler_params=pltpu.CompilerParams(vmem_limit_bytes=8 * MIB),
    )(*args)


def step_kernel(last, *refs):
    (moved, stress, faces, velocity, rigidity, buoyancy) = refs[:6]
    (sigma_star, sigma_zero, friction) = refs[6:9]
    (received, near, far, depth_own, depth_near, depth_far, own) = refs[9:16]
    refs = refs[16:]
    nodes, ny, width = velocity.shape
    chunks = nodes // CHUNK
    fault = ny // 2 - 1
    scale = courant * 0.5
    copies = []
    if last:
        results, (velocity_new, shear, tips, broken, state_new, bounds), sems = (
            refs[:5],
            refs[5:11],
            refs[11],
        )

        def send(source, target):
            copies.append(pltpu.make_async_copy(source, target, sems.at[len(copies)]))
            copies[-1].start()

        inner = pl.ds(1, nodes - 2)
        send(stress.at[0, inner], results[1].at[0, inner])
        base = fault * nodes
        send(faces.at[pl.ds(0, base)], results[2].at[pl.ds(0, base)])
        above = pl.ds(base + nodes, (ny - 2 - fault) * nodes)
        send(faces.at[above], results[2].at[above])
    else:
        later, lead = refs[:2]
        velocity_new, stress_new, faces_new, state_new, core, own_new, edges = refs[2:9]
        edges_sent = refs[9]
        shear = stress_new.at[1]
    even, chip_even, _ = parities()

    def level_of(ref, y):
        return ref.reshape(nodes * ny, width)[pl.ds(y, nodes, stride=ny), :]

    near_parts, far_parts = unpacked(near, nodes), unpacked(far, nodes)
    traction = []
    for surface in range(2):
        base = surface * 2 * nodes
        mate = lax.select(
            even, received[base : base + nodes], received[base + nodes : base + 2 * nodes]
        )
        traction.append(
            own[surface, nodes : 2 * nodes] + mate + (near_parts[surface] + far_parts[surface])
        )

    near_halo, far_halo = (jnp.concatenate(x[2:], axis=0) for x in (near_parts, far_parts))
    left = lax.select(
        even, lax.select(chip_even, far_halo, near_halo), received[4 * nodes + 48 :]
    )
    right = lax.select(
        even, received[4 * nodes : 4 * nodes + 48], lax.select(chip_even, near_halo, far_halo)
    )
    stress_left = left[32:] + scale * left[16:32] * velocity[0]
    stress_right = right[32:] - scale * right[16:32] * velocity[nodes - 1]
    added_left = -scale * rigidity[0] * left[:16]
    added_right = scale * rigidity[nodes - 1] * right[:16]

    shape = (CHUNK, ny, width)
    sides = depth_sides(depth_own[...], depth_near[...], depth_far[...], chunks).reshape(shape)
    lane = lane_of(shape)
    edge = (lane == 0) | (lane == width - 1)
    margin = (lane < 2) | (lane >= width - 2)

    for at in range(0, nodes, CHUNK):
        cells = slice(at, at + CHUNK)
        place = 8 * (at // CHUNK)
        extra = jnp.where(margin, turned(sides, -(place + 2)), 0.0)
        velocity_new[cells] = moved[cells] + courant * buoyancy[cells] * extra
        extra = jnp.where(edge, turned(sides, -(place + 5)), 0.0)
        shear[cells] = stress[1, cells] + extra
        if last and (at + CHUNK) % (nodes // 2) == 0:
            half = pl.ds(at + CHUNK - nodes // 2, nodes // 2)
            send(shear.at[half], results[1].at[1, half])

    first_row, last_row = stress[0, 0] + added_left, stress[0, nodes - 1] + added_right
    if last:
        tips[0], tips[1] = first_row, last_row
        send(tips.at[0], results[1].at[0, 0])
        send(tips.at[1], results[1].at[0, nodes - 1])

    row = lax.broadcasted_iota(jnp.int32, (nodes, width), 0)
    lower, upper = slice(fault, fault + 1), slice(fault + 1, fault + 2)
    across = level_of(stress.at[0], fault + 1) - level_of(stress.at[0], fault)
    across = across + jnp.where(row == 0, added_left[upper] - added_left[lower], 0.0)
    across = across + jnp.where(row == nodes - 1, added_right[upper] - added_right[lower], 0.0)
    slip_rate = level_of(velocity, fault + 1) - level_of(velocity, fault)
    normal = sigma_zero[...] + bimaterial * jnp.tanh(across)
    state = normal + (sigma_star[...] - normal) * jnp.exp(
        -(jnp.abs(slip_rate) + slip_ref) * decay_rate
    )
    state_new[...] = state
    strength = friction[...] * state
    trial = faces[fault * nodes : (fault + 1) * nodes] if last else level_of(faces, fault)
    clipped = jnp.clip(trial, -strength, strength)
    bottom = traction[0] + impedance * level_of(velocity, 0)
    top = traction[1] - impedance * level_of(velocity, ny - 1)
    if last:
        broken[...] = clipped
        bounds[0], bounds[1] = bottom, top
        send(broken, results[2].at[pl.ds(fault * nodes, nodes)])
        send(state_new, results[3])
        send(bounds, results[4])
    else:
        stress_new[0, 0], stress_new[0, nodes - 1] = first_row, last_row
        faces_new.reshape(nodes * ny, width)[pl.ds(fault, nodes, stride=ny), :] = clipped

    flat = velocity_new.reshape(nodes * ny, width)
    for y, change in (
        (fault, clipped - trial),
        (fault + 1, trial - clipped),
        (0, -bottom),
        (ny - 1, top),
    ):
        at = pl.ds(y, nodes, stride=ny)
        flat[at, :] = flat[at, :] + courant * level_of(buoyancy, y) * change
    for x, change in (
        (0, -stress_left),
        (1, -added_left),
        (nodes - 2, added_right),
        (nodes - 1, stress_right),
    ):
        velocity_new[x] = velocity_new[x] + (0.5 * courant) * buoyancy[x] * change

    if last:
        send(velocity_new, results[0])
        for copy in copies:
            copy.wait()
        return

    for surface in range(2):
        fresh = level_of(velocity_new, surface * (ny - 1)).astype(jnp.bfloat16)
        total = later[surface] + jnp.dot(
            lead[surface], fresh, preferred_element_type=jnp.float32
        )
        deal(total, core, own_new, surface)
    strike_edge(
        core, 4 * nodes, velocity_new[0], rigidity[0], stress_new[0, 0], velocity_new[1], 1.0
    )
    strike_edge(
        core,
        4 * nodes + 48,
        velocity_new[nodes - 1],
        rigidity[nodes - 1],
        stress_new[0, nodes - 1],
        velocity_new[nodes - 2],
        -1.0,
    )
    cells = [slice(at, at + CHUNK) for at in range(0, nodes, CHUNK)]
    depth_edges(edges, edges_sent, [(velocity_new[c], stress_new[1, c], rigidity[c]) for c in cells])


def step_call(last, *args):
    nodes, ny, width = args[0].shape
    f32 = jnp.float32
    shapes = [(nodes, ny, width), (2, nodes, ny, width)]
    if last:
        shapes += [(nodes * (ny - 1), width), (nodes, width), (2, nodes, width)]
        held = [(nodes, ny, width)] * 2 + [(2, ny, width), (nodes, width), *shapes[3:]]
        scratch = [pltpu.VMEM(shape, f32) for shape in held]
        scratch += [pltpu.SemaphoreType.DMA((11,))]
        space = pltpu.HBM
    else:
        shapes += [
            (nodes, ny, width),
            (nodes, width),
            (4 * nodes + 96, width),
            (2, 3 * nodes, width),
            (8, nodes * ny),
        ]
        scratch, space = [], pltpu.VMEM
    out_shape = [jax.ShapeDtypeStruct(shape, f32) for shape in shapes]
    if not last:
        out_shape.append(jax.ShapeDtypeStruct((nodes, width), jnp.bfloat16))
    return pl.pallas_call(
        functools.partial(step_kernel, last),
        out_shape=out_shape,
        input_output_aliases={} if last else {1: 1, 2: 2},
        out_specs=[pl.BlockSpec(memory_space=space)] * len(out_shape),
        scratch_shapes=scratch,
        compiler_params=pltpu.CompilerParams(vmem_limit_bytes=16 * MIB),
    )(*args)


def exchange(core, own, edges, edges_sent):
    received = lax.ppermute(core, GX, swap_pairs(GX, 1, 0))
    depth_near = lax.ppermute(edges_sent, GZ, swap_pairs(GZ, 1, 0))
    far = lax.ppermute(relay_call(False, received, own), GX, swap_pairs(GX, 2, 2))
    near = relay_call(True, received, own, depth_near)
    near = lax.ppermute(near, GX, swap_pairs(GX, 2, 0))
    depth_far = lax.ppermute(depth_near, GZ, onward_pairs(GZ))
    return received, near, far, edges, depth_near, depth_far


def local(
    velocity,
    stress_xz,
    stress_y,
    rigidity,
    buoyancy,
    sigma_star,
    sigma_zero,
    friction,
    history,
    kernel,
    cone,
):
    surfaces, lags, nodes, width = history.shape
    faces = stress_y.shape[1]
    past = history.reshape(surfaces, lags * nodes, width)
    matrix = kernel.reshape(surfaces, -1, kernel.shape[3])
    turned_cone = jnp.transpose(cone, (0, 2, 3, 1))
    face_rows = jnp.transpose(stress_y, (1, 0, 2)).reshape(faces * nodes, width)
    core, own, later, lead, edges, sent, velocity, stress_xz, rigidity, *rest = first_call(
        velocity,
        stress_xz,
        rigidity,
        turned_cone,
        past,
        matrix,
        face_rows,
        buoyancy,
        sigma_star,
        sigma_zero,
        friction,
    )
    face_rows, buoyancy, sigma_star, sigma_zero, friction = rest
    *inner, stiffness = inner_call(False, velocity, stress_xz, face_rows, rigidity, buoyancy)
    velocity, stress_xz, stress_y, state, core, own, edges, sent = step_call(
        False,
        *inner,
        velocity,
        rigidity,
        buoyancy,
        sigma_star,
        sigma_zero,
        friction,
        *exchange(core, own, edges, sent),
        own,
        later,
        lead,
    )
    inner = inner_call(True, velocity, stress_xz, stress_y, rigidity, buoyancy, stiffness)
    velocity, stress_xz, face_rows, state, bounds = step_call(
        True,
        *inner,
        velocity,
        rigidity,
        buoyancy,
        state,
        sigma_zero,
        friction,
        *exchange(core, own, edges, sent),
        own,
    )
    stress_y = jnp.transpose(face_rows.reshape(faces, nodes, width), (1, 0, 2))
    return velocity, stress_xz, stress_y, state, bounds


def solution(mesh):
    in_specs = (
        P("gx", None, "gz"),
        P(None, "gx", None, "gz"),
        P("gx", None, "gz"),
        P("gx", None, "gz"),
        P("gx", None, "gz"),
        P("gx", "gz"),
        P("gx", "gz"),
        P("gx", "gz"),
        P(None, None, "gx", "gz"),
        P(),
        P(),
    )
    out_specs = (
        P("gx", None, "gz"),
        P(None, "gx", None, "gz"),
        P("gx", None, "gz"),
        P("gx", "gz"),
        P(None, "gx", "gz"),
    )
    return jax.shard_map(
        local, mesh=mesh, in_specs=in_specs, out_specs=tuple(out_specs), check_vma=False
    )
```
